128 devices in a mesh: dp: 32 (over z, y, core), group: 4 (over x).
Axes of the slice: x: 4, y: 4, z: 4, core: 2. Of those that a mesh axis runs over, the one named last changes fastest.
Arguments:
- activations: bfloat16 [8192, 8192], P('dp'), may hold values from -6 to 6
- cotangent: bfloat16 [8192, 2048], P('dp'), may hold values from -6 to 6
- owner_table: int32 [16], replicated, may hold values from 0 to 15, each once
- statistics: float32 [32, 1024, 1024], P('dp'), may hold values from -1 to 2, as said below
- warm_roots: float32 [32, 1024, 1024], P('dp'), may hold values from -1 to 2
Outputs:
- new_statistics: float32 [32, 1024, 1024], P('dp')
- new_roots: float32 [32, 1024, 1024], P('dp')
- update: bfloat16 [32, 512, 1024], P('dp', 'group')
The draws below stay inside these ranges and needn't reach their ends.
Inputs may be any that keep to these rules, and one draw needn't show every extreme that they name: `statistics`: each matrix is symmetric.
All inputs are finite; a program needn't handle non-finite values.
Results may differ from the reference program's by a relative error of at most 0.001.
Values may be sent and summed in bfloat16 or wider, within the bound.
No kernel may reach another device: no remote copies, remote signals or barrier semaphores. Data moves between devices by JAX's collectives and lax.ppermute only.
A program may use at most 192 MiB of HBM per device.

```python
import math
import jax
import jax.numpy as jnp
from jax import lax

BS = 1024
F = 2048
ITERS = 2
D_IN = 8192
BLOCKS = 16
TOKENS = 8192


STAT_DECAY = 0.95


def uniform_base(key):
    return jax.random.uniform(key, (2 * BLOCKS, BS), jnp.float32)


def draw_statistics(key, part):
    base_values = uniform_base(key)
    key = jax.random.fold_in(key, 11)
    diagonal = 2.0 ** base_values
    spread = 0.2
    scatter_noise = jax.random.uniform(key, (2 * BLOCKS, BS, BS), jnp.float32, -1.0, 1.0) * (spread / BS ** 0.5)
    symmetric = 0.5 * (scatter_noise + jnp.swapaxes(scatter_noise, 1, 2))
    identity = jnp.eye(BS, dtype=jnp.float32)
    return symmetric * (1.0 - identity) + diagonal[:, :, None] * identity


def draw_warm_roots(key, part):
    base_values = uniform_base(key)
    key = jax.random.fold_in(key, 23)
    diagonal = 2.0 ** base_values
    gain_key, off_key = jax.random.split(key)
    gain_factor = 1.0 + 0.15 * jax.random.uniform(gain_key, (2 * BLOCKS, BS), jnp.float32, -1.0, 1.0)
    diag_level = (STAT_DECAY * diagonal + (1.0 - STAT_DECAY)) ** (-0.25) * gain_factor
    off_entries = jax.random.uniform(off_key, (2 * BLOCKS, BS, BS), jnp.float32, -1.0, 1.0) * (0.04 / BS ** 0.5)
    identity = jnp.eye(BS, dtype=jnp.float32)
    return off_entries * (1.0 - identity) + diag_level[:, :, None] * identity


def level_of(key, shape, cuts, least, top_value):
    level = 1.0
    for position, shards_of in cuts:
        draws = jax.random.uniform(jax.random.fold_in(jax.random.fold_in(key, 6), position), (shards_of,), jnp.float32, least / len(cuts), top_value / len(cuts))
        level = level * jnp.repeat(jnp.exp(draws), shape[position] // shards_of).reshape((-1,) + (1,) * (len(shape) - 1 - position))
    return level


def noise(key, extent, deviation, most, pieces=(), held_as=jnp.bfloat16):
    gain = level_of(key, extent, pieces, -0.22, 0.18) if pieces else 1.0
    values = jax.random.normal(key, extent, jnp.float32) * deviation * gain
    return jnp.minimum(jnp.maximum(values, -most), most).astype(held_as)


def setup_inputs(seed: int = 0) -> dict:
    seeds = jax.random.split(jax.random.key(seed), 6)
    activations = noise(seeds[0], (TOKENS, D_IN), 1.0, 6.0, ((0, 32),))
    cotangent = noise(seeds[1], (TOKENS, F), 1.0, 6.0, ((0, 32),))
    owner_table = jax.random.permutation(seeds[2], BLOCKS).astype(jnp.int32)
    statistics = draw_statistics(jax.random.fold_in(seeds[5], 71), 0)
    warm_roots = draw_warm_roots(jax.random.fold_in(seeds[5], 71), 0)
    return {"activations": activations, "cotangent": cotangent, "owner_table": owner_table, "statistics": statistics, "warm_roots": warm_roots}


STAT_DECAY = 0.95
HIGHEST_PREC = lax.Precision.HIGHEST

def product(left_side, right_side):
    return jnp.dot(left_side, right_side, precision=HIGHEST_PREC, preferred_element_type=jnp.float32)

def newton(inv_root, statistic):
    for iteration in range(ITERS):
        squared = product(inv_root, inv_root)
        fourth = product(squared, squared)
        fifth = product(fourth, inv_root)
        inv_root = (5.0 * inv_root - product(fifth, statistic)) * 0.25
    return inv_root

def reference(activations, cotangent, owner_table, statistics, warm_roots):
    grad_scale = 1.0 / math.sqrt(TOKENS)
    feature_blocks = D_IN // BS

    def slot_work(slot_index):
        block_id = owner_table[slot_index]
        out_start = (block_id // feature_blocks * BS).astype(jnp.int32)
        in_start = (block_id % feature_blocks * BS).astype(jnp.int32)
        dy_cols = lax.dynamic_slice_in_dim(cotangent, out_start, BS, 1)
        x_cols = lax.dynamic_slice_in_dim(activations, in_start, BS, 1)
        gradient = jnp.einsum('tr,tc->rc', dy_cols, x_cols, preferred_element_type=jnp.float32) * grad_scale
        left_stat = STAT_DECAY * statistics[2 * slot_index] + (1.0 - STAT_DECAY) / BS * product(gradient, gradient.T)
        right_stat = STAT_DECAY * statistics[2 * slot_index + 1] + (1.0 - STAT_DECAY) / BS * product(gradient.T, gradient)
        left_root = newton(warm_roots[2 * slot_index], left_stat)
        right_root = newton(warm_roots[2 * slot_index + 1], right_stat)
        update = product(product(left_root, gradient), right_root).astype(jnp.bfloat16)
        return (jnp.stack([left_stat, right_stat]), jnp.stack([left_root, right_root]), update)
    stats_out, roots_out, updates = lax.map(slot_work, jnp.arange(BLOCKS, dtype=jnp.int32))
    return (stats_out.reshape(2 * BLOCKS, BS, BS), roots_out.reshape(2 * BLOCKS, BS, BS), updates.reshape(2 * BLOCKS, BS // 2, BS))
```

```python
import functools
import math

import jax
import jax.numpy as jnp
from jax import lax
from jax.experimental import pallas as pl
from jax.experimental.pallas import tpu as pltpu
from jax.sharding import PartitionSpec as P

ITERS = 2
STAT_DECAY = 0.95

BF16 = jnp.bfloat16
F32 = jnp.float32
I16 = jnp.int16
VMEM = pl.BlockSpec(memory_space=pltpu.VMEM)
SMEM = pl.BlockSpec(memory_space=pltpu.SMEM)
HBM = pl.BlockSpec(memory_space=pl.ANY)

BS = 1024
QUARTER = BS // 4
HALF = BS // 2
SUB = QUARTER // 2
TAIL = 16
STEPS = 128.0
TOP = 32767.0


def params(mib):
    return pltpu.CompilerParams(vmem_limit_bytes=mib * 2**20)


def cost(flops, bytes_accessed):
    return pl.CostEstimate(flops=flops, bytes_accessed=bytes_accessed, transcendentals=0)


def dot(a, b):
    return jnp.dot(a, b, preferred_element_type=F32)


def dot_nt(a, b):
    return lax.dot_general(a, b, (((1,), (1,)), ((), ())), preferred_element_type=F32)


def split(value):
    high = value.astype(BF16)
    return high, (value - high.astype(F32)).astype(BF16)


def pack(value):
    level = jnp.maximum(jnp.max(jnp.abs(value), axis=0, keepdims=True), 1e-32)
    code = jnp.floor(jnp.log2(level) * STEPS) + 2.0
    fixed = jnp.round(value * (TOP * jnp.exp2(code * (-1.0 / STEPS))))
    return fixed.astype(jnp.int32).astype(I16), code


def pack_codes(codes):
    row = lax.broadcasted_iota(jnp.int32, (TAIL, codes[0].shape[1]), 0)
    out = jnp.zeros((TAIL, codes[0].shape[1]), F32)
    for index, code in enumerate(codes):
        out = jnp.where(row == index, code, out)
    return out.astype(jnp.int32).astype(I16)


def unpack_scales(tail):
    return jnp.exp2(tail.astype(jnp.int32).astype(F32) * (1.0 / STEPS)) * (1.0 / TOP)


def unpack(fixed, scale):
    return fixed.astype(jnp.int32).astype(F32) * scale


def partial_kernel(scale, owner, place, act, act_other, cot, cot_other, *rest):
    along = (rest[0:4], rest[4:8])
    turned = rest[8]
    z, y, core = place[0], place[1], place[2]
    for half in range(2):
        cols = slice(half * QUARTER, (half + 1) * QUARTER)
        turned[half, :, :QUARTER] = cot[:, cols].astype(F32).T.astype(BF16)
        turned[half, :, QUARTER:] = cot_other[:, cols].astype(F32).T.astype(BF16)
    codes = {}
    for step_y in range(4):
        for step_z in range(4):
            slot = ((z + step_z) % 4) * 4 + (y + step_y) % 4
            block = owner[slot]
            out_half, in_block = block // 8, block % 8
            own_cols = pl.ds(pl.multiple_of(in_block * BS + core * HALF, HALF), HALF)
            other_cols = pl.ds(pl.multiple_of(in_block * HALF, HALF), HALF)
            rows = turned[out_half]
            term = dot(rows[:, :QUARTER], act[:, own_cols])
            term = (term + dot(rows[:, QUARTER:], act_other[:, other_cols])) * scale
            for way, (to, position) in enumerate(((step_y, step_z), (step_z, step_y))):
                part = term[way * SUB : (way + 1) * SUB]
                where = slice(position * SUB, (position + 1) * SUB)
                if to == 0:
                    along[way][0][where, :] = part
                else:
                    fixed, code = pack(part)
                    along[way][to][where, :] = fixed
                    codes[way, to, position] = code
    for way in range(2):
        for to in range(1, 4):
            along[way][to][4 * SUB :, :] = pack_codes([codes[way, to, p] for p in range(4)])


def partial_sums(scale, owner, place, act, act_other, cot, cot_other):
    own = jax.ShapeDtypeStruct((4 * SUB, HALF), F32)
    sent = jax.ShapeDtypeStruct((4 * SUB + TAIL, HALF), I16)
    return pl.pallas_call(
        functools.partial(partial_kernel, scale),
        out_shape=[own, sent, sent, sent] * 2,
        in_specs=[SMEM, SMEM, VMEM, VMEM, VMEM, VMEM],
        out_specs=[VMEM] * 8,
        scratch_shapes=[pltpu.VMEM((2, QUARTER, 2 * QUARTER), BF16)],
        compiler_params=params(32),
        cost_estimate=cost(2 * 512 * 512 * 4096, 13 * 2**20),
        name="partial_sums",
    )(owner, place, act, act_other, cot, cot_other)


def middle_kernel(*refs):
    ins, outs = (refs[0:4], refs[4:8]), (refs[8:12], refs[12:16])
    for way in range(2):
        own, arrived = ins[way][0], ins[way][1:]
        scales = [unpack_scales(a[4 * SUB :, :]) for a in arrived]
        for position in range(4):
            where = slice(position * SUB, (position + 1) * SUB)
            total = own[where, :]
            for a, s in zip(arrived, scales):
                total = total + unpack(a[where, :], s[position : position + 1, :])
            if position == 0:
                outs[way][0][...] = total
            else:
                fixed, code = pack(total)
                outs[way][position][:SUB, :] = fixed
                outs[way][position][SUB:, :] = pack_codes([code])


def middle_sums(first, second):
    own = jax.ShapeDtypeStruct((SUB, HALF), F32)
    sent = jax.ShapeDtypeStruct((SUB + TAIL, HALF), I16)
    return pl.pallas_call(
        middle_kernel,
        out_shape=[own, sent, sent, sent] * 2,
        in_specs=[VMEM] * 8,
        out_specs=[VMEM] * 8,
        compiler_params=params(32),
        cost_estimate=cost(2**20, 8 * 2**20),
        name="middle_sums",
    )(*first, *second)


def last_kernel(*refs):
    out = refs[8]
    parts = []
    for way in range(2):
        total = refs[4 * way][...]
        for a in refs[4 * way + 1 : 4 * way + 4]:
            scale = unpack_scales(a[SUB:, :])[0:1, :]
            total = total + unpack(a[:SUB, :], scale)
        parts.append(total)
    fixed, code = pack(jnp.concatenate(parts, 0))
    out[:QUARTER, :] = fixed
    out[QUARTER:, :] = pack_codes([code])


def last_sums(first, second):
    return pl.pallas_call(
        last_kernel,
        out_shape=jax.ShapeDtypeStruct((QUARTER + TAIL, HALF), I16),
        in_specs=[VMEM] * 8,
        out_specs=VMEM,
        compiler_params=params(32),
        cost_estimate=cost(2**20, 2 * 2**20),
        name="last_sums",
    )(*first, *second)


ROW_TILE = 512
COL_TILE = 256


def matmul(left, right, store, transposed=False, rows=BS):
    left_high, left_low = left
    right_high, right_low = right
    times = dot_nt if transposed else dot
    tile = min(rows, ROW_TILE)

    def step(index, carry):
        at = pl.ds(pl.multiple_of(index * tile, tile), tile)
        for col in range(BS // COL_TILE):
            cols = slice(col * COL_TILE, (col + 1) * COL_TILE)
            pick = (cols, slice(None)) if transposed else (slice(None), cols)
            value = times(left_high[at, :], right_low[pick])
            value = value + times(left_low[at, :], right_high[pick])
            value = value + times(left_high[at, :], right_high[pick])
            store(at, cols, value)
        return carry

    lax.fori_loop(0, rows // tile, step, 0)


def split_into(target):
    def store(at, cols, value):
        target[0][at, cols], target[1][at, cols] = split(value)

    return store


def split_block(source, target):
    def step(index, carry):
        at = pl.ds(pl.multiple_of(index * 128, 128), 128)
        target[0][at, :], target[1][at, :] = split(source[at, :])
        return carry

    lax.fori_loop(0, BS // 128, step, 0)


def fifth_kernel(root, high, low, root_high, root_low, power_high, power_low):
    x, out, power = (root_high, root_low), (high, low), (power_high, power_low)
    split_block(root, x)
    matmul(x, x, split_into(out))
    matmul(out, out, split_into(power))
    matmul(power, x, split_into(out))


def fifth_power(root):
    block = jax.ShapeDtypeStruct((BS, BS), BF16)
    return pl.pallas_call(
        fifth_kernel,
        out_shape=[block, block],
        in_specs=[VMEM],
        out_specs=[VMEM, VMEM],
        scratch_shapes=[pltpu.VMEM((BS, BS), BF16)] * 4,
        compiler_params=params(48),
        cost_estimate=cost(9 * 2 * BS**3, 8 * 2**20),
        name="fifth_power",
    )(root)


def newton_kernel(place, pieces, other, stat_in, root_in, high_in, low_in, stat_out, root_out,
                  left_out, g_high, g_low, a_high, a_low, b_high, b_low, s_high, s_low, f, x, sems):
    core, group = place[2], place[3]
    grad, a, b, stat = (g_high, g_low), (a_high, a_low), (b_high, b_low), (s_high, s_low)
    copies = [
        pltpu.make_async_copy(source, target, sems.at[index])
        for index, (source, target) in enumerate(
            ((stat_in, f), (high_in, a_high), (low_in, a_low), (root_in, x))
        )
    ]
    for copy in copies:
        copy.start()

    for source, half in ((pieces, core), (other, 1 - core)):
        along_cols = pl.ds(pl.multiple_of(half * HALF, HALF), HALF)
        for shift in range(4):
            quarter = (group - shift + 4) % 4
            along_rows = pl.ds(pl.multiple_of(quarter * QUARTER, QUARTER), QUARTER)
            scale = unpack_scales(source[shift, QUARTER:, :])[0:1, :]
            value = unpack(source[shift, :QUARTER, :], scale)

            @pl.when(core == 0)
            def _():
                g_high[along_rows, along_cols], g_low[along_rows, along_cols] = split(value)

            @pl.when(core == 1)
            def _():
                turned = value.T
                g_high[along_cols, along_rows], g_low[along_cols, along_rows] = split(turned)

    copies[0].wait()

    def store_stat(at, cols, value):
        new = STAT_DECAY * f[at, cols] + (1.0 - STAT_DECAY) / BS * value
        f[at, cols] = new
        s_high[at, cols], s_low[at, cols] = split(new)

    matmul(grad, grad, store_stat, transposed=True)
    stat_copy = pltpu.make_async_copy(f, stat_out, sems.at[4])
    stat_copy.start()
    for copy in copies[1:]:
        copy.wait()

    def store_first(at, cols, value):
        new = (5.0 * x[at, cols] - value) * 0.25
        x[at, cols] = new
        b_high[at, cols], b_low[at, cols] = split(new)

    matmul(a, stat, store_first)
    matmul(b, b, split_into(a))
    stat_copy.wait()

    def store_fourth(at, cols, value):
        f[at, cols] = value

    matmul(a, a, store_fourth)
    split_block(f, a)
    matmul(a, b, store_fourth)
    split_block(f, a)

    def store_root(at, cols, value):
        new = (5.0 * x[at, cols] - value) * 0.25
        x[at, cols] = new
        b[0][at, cols], b[1][at, cols] = split(new)

    matmul(a, stat, store_root)
    root_copy = pltpu.make_async_copy(x, root_out, sems.at[5])
    root_copy.start()

    @pl.when(core == 0)
    def _():
        for side in range(2):
            first = pl.multiple_of(side * (BS // 2) + group * SUB, SUB)
            rows = pl.ds(first, SUB)
            for half in range(2):
                a[half][side * SUB : (side + 1) * SUB, :] = b[half][rows, :]

        def store_left(at, cols, value):
            left_out[at, cols] = value

        matmul(a, grad, store_left, rows=2 * SUB)

    root_copy.wait()


def newton(place, pieces, other, stat, root, high, low):
    block = jax.ShapeDtypeStruct((BS, BS), F32)
    half = pltpu.VMEM((BS, BS), BF16)
    full = pltpu.VMEM((BS, BS), F32)
    return pl.pallas_call(
        newton_kernel,
        out_shape=[block, block, jax.ShapeDtypeStruct((2 * SUB, BS), F32)],
        in_specs=[SMEM, VMEM, VMEM, HBM, HBM, HBM, HBM],
        out_specs=[HBM, HBM, VMEM],
        scratch_shapes=[half] * 8 + [full, full, pltpu.SemaphoreType.DMA((6,))],
        compiler_params=params(56),
        cost_estimate=cost(18 * 2 * BS**3, 24 * 2**20),
        name="newton",
    )(place, pieces, other, stat, root, high, low)


def update_kernel(place, left, root, out, l_high, l_low, r_high, r_low):
    @pl.when(place[2] == 1)
    def _():
        l_high[...], l_low[...] = split(left[...])
        split_block(root, (r_high, r_low))

        def store(at, cols, value):
            out[at, cols] = value.astype(BF16)

        matmul((l_high, l_low), (r_high, r_low), store, rows=2 * SUB)


def update_rows(place, left, root):
    return pl.pallas_call(
        update_kernel,
        out_shape=jax.ShapeDtypeStruct((2 * SUB, BS), BF16),
        in_specs=[SMEM, VMEM, VMEM],
        out_specs=VMEM,
        scratch_shapes=[pltpu.VMEM((2 * SUB, BS), BF16)] * 2 + [pltpu.VMEM((BS, BS), BF16)] * 2,
        compiler_params=params(32),
        cost_estimate=cost(3 * 2 * 2 * SUB * BS * BS, 6 * 2**20),
        name="update_rows",
    )(place, left, root)


def route(step_z, step_y, swap=False):
    pairs = []
    for z in range(4):
        for y in range(4):
            for core in range(2):
                source = (z * 4 + y) * 2 + core
                target = ((z + step_z) % 4 * 4 + (y + step_y) % 4) * 2 + (1 - core if swap else core)
                pairs.append((source, target))
    return pairs


def body(activations, cotangent, owner_table, statistics, warm_roots):
    dp, group = lax.axis_index("dp"), lax.axis_index("group")
    core, y, z = dp % 2, dp // 2 % 4, dp // 8
    place = jnp.stack([z, y, core, group]).astype(jnp.int32)
    scale = 1.0 / math.sqrt(activations.shape[0] * lax.axis_size("dp"))

    def swap(value):
        return lax.ppermute(value, "dp", route(0, 0, swap=True))

    act_sent = jnp.concatenate(
        [lax.dynamic_slice_in_dim(activations, i * BS + (1 - core) * HALF, HALF, 1) for i in range(8)], 1
    )
    cot = jnp.concatenate(
        [lax.dynamic_slice_in_dim(cotangent, o * BS + group * QUARTER, QUARTER, 1) for o in range(2)], 1
    )
    act_other, cot_other = swap(act_sent), swap(cot)
    out = partial_sums(scale, owner_table, place, activations, act_other, cot, cot_other)

    def along_y(value, step):
        return lax.ppermute(value, "dp", route(0, step))

    def along_z(value, step):
        return lax.ppermute(value, "dp", route(step, 0))

    first = [out[0]] + [along_y(out[step], step) for step in range(1, 4)]
    second = [out[4]] + [along_z(out[4 + step], step) for step in range(1, 4)]
    out = middle_sums(first, second)
    first = [out[0]] + [along_z(out[step], step) for step in range(1, 4)]
    second = [out[4]] + [along_y(out[4 + step], step) for step in range(1, 4)]
    piece = last_sums(first, second)

    pieces = [piece]
    for step in range(1, 4):
        pieces.append(lax.ppermute(piece, "group", [(i, (i + step) % 4) for i in range(4)]))
    pieces = jnp.stack(pieces)
    other = swap(pieces)

    high, low = fifth_power(warm_roots[0])
    statistic, root, left = newton(place, pieces, other, statistics[0], warm_roots[0], high, low)
    left = lax.ppermute(left, "dp", [(2 * k, 2 * k + 1) for k in range(16)])
    rows = update_rows(place, left, root)
    back = lax.ppermute(rows[:SUB], "dp", [(2 * k + 1, 2 * k) for k in range(16)])
    update = jnp.where(core == 0, back, rows[SUB:])
    return (statistic[None], root[None], update[None])


def solution(mesh):
    in_specs = (P("dp", None), P("dp", None), P(), P("dp", None, None), P("dp", None, None))
    out_specs = (P("dp", None, None), P("dp", None, None), P("dp", "group", None))
    return jax.shard_map(body, mesh=mesh, in_specs=in_specs, out_specs=out_specs, check_vma=False)
```

```python
import functools
import math

import jax
import jax.numpy as jnp
from jax import lax
from jax.experimental import pallas as pl
from jax.experimental.pallas import tpu as pltpu
from jax.sharding import PartitionSpec as P

ITERS = 2
STAT_DECAY = 0.95

BF16 = jnp.bfloat16
F32 = jnp.float32
I16 = jnp.int16
VMEM = pl.BlockSpec(memory_space=pltpu.VMEM)
SMEM = pl.BlockSpec(memory_space=pltpu.SMEM)
HBM = pl.BlockSpec(memory_space=pltpu.HBM)
ANY = pl.BlockSpec(memory_space=pl.ANY)

BS = 1024
QUARTER = BS // 4
HALF = BS // 2
SUB = QUARTER // 2
TAIL = 16
STEPS = 128.0
TOP = 32767.0


def params(mib):
    return pltpu.CompilerParams(vmem_limit_bytes=mib * 2**20)


def cost(flops, bytes_accessed):
    return pl.CostEstimate(flops=flops, bytes_accessed=bytes_accessed, transcendentals=0)


def dot(a, b):
    return jnp.dot(a, b, preferred_element_type=F32)


def dot_nt(a, b):
    return lax.dot_general(a, b, (((1,), (1,)), ((), ())), preferred_element_type=F32)


def split(value):
    high = value.astype(BF16)
    return high, (value - high.astype(F32)).astype(BF16)


def pack(value):
    level = jnp.maximum(jnp.max(jnp.abs(value), axis=0, keepdims=True), 1e-32)
    code = jnp.floor(jnp.log2(level) * STEPS) + 2.0
    fixed = jnp.round(value * (TOP * jnp.exp2(code * (-1.0 / STEPS))))
    return fixed.astype(jnp.int32).astype(I16), code


def pack_codes(codes):
    row = lax.broadcasted_iota(jnp.int32, (TAIL, codes[0].shape[1]), 0)
    out = jnp.zeros((TAIL, codes[0].shape[1]), F32)
    for index, code in enumerate(codes):
        out = jnp.where(row == index, code, out)
    return out.astype(jnp.int32).astype(I16)


def unpack_scales(tail):
    return jnp.exp2(tail.astype(jnp.int32).astype(F32) * (1.0 / STEPS)) * (1.0 / TOP)


def unpack(fixed, scale):
    return fixed.astype(jnp.int32).astype(F32) * scale


def fetch_kernel(place, act, cot, sent, cot_out, sems):
    core, group = place[2], place[3]
    copies = []
    for block in range(8):
        source = act.at[:, pl.ds(pl.multiple_of(block * BS + (1 - core) * HALF, HALF), HALF)]
        copies.append((source, sent.at[:, block * HALF : (block + 1) * HALF]))
    for block in range(2):
        source = cot.at[:, pl.ds(pl.multiple_of(block * BS + group * QUARTER, QUARTER), QUARTER)]
        copies.append((source, cot_out.at[:, block * QUARTER : (block + 1) * QUARTER]))
    copies = [pltpu.make_async_copy(s, t, sems.at[i]) for i, (s, t) in enumerate(copies)]
    for copy in copies:
        copy.start()
    for copy in copies:
        copy.wait()


def fetch(place, act, cot):
    return pl.pallas_call(
        fetch_kernel,
        out_shape=[
            jax.ShapeDtypeStruct((act.shape[0], act.shape[1] // 2), BF16),
            jax.ShapeDtypeStruct((cot.shape[0], 2 * QUARTER), BF16),
        ],
        in_specs=[SMEM, HBM, HBM],
        out_specs=[VMEM] * 2,
        scratch_shapes=[pltpu.SemaphoreType.DMA((10,))],
        compiler_params=params(60),
        cost_estimate=cost(0, 5 * 2**20),
        name="fetch",
    )(place, act, cot)


def partial_kernel(scale, owner, place, act, act_other, cot, cot_other, own, *rest):
    sent, turned = rest[:3], rest[3]
    z, y, core = place[0], place[1], place[2]
    for half in range(2):
        cols = slice(half * QUARTER, (half + 1) * QUARTER)
        turned[half, :, :QUARTER] = cot[:, cols].astype(F32).T.astype(BF16)
        turned[half, :, QUARTER:] = cot_other[:, cols].astype(F32).T.astype(BF16)
    for first in range(4):
        codes = []
        for second in range(4):
            step_y = jnp.where(core == 0, first, second)
            step_z = jnp.where(core == 0, second, first)
            block = owner[(z + step_z) % 4 * 4 + (y + step_y) % 4]
            out_half, in_block = block // 8, block % 8
            own_cols = pl.ds(pl.multiple_of(in_block * BS + core * HALF, HALF), HALF)
            cols = pl.ds(pl.multiple_of(in_block * HALF, HALF), HALF)
            rows = turned[out_half]
            term = dot(rows[:, :QUARTER], act[:, own_cols])
            term = (term + dot(rows[:, QUARTER:], act_other[:, cols])) * scale
            where = slice(second * QUARTER, (second + 1) * QUARTER)
            if first == 0:
                own[where, :] = term
            else:
                fixed, code = pack(term)
                sent[first - 1][where, :] = fixed
                codes.append(code)
        if first > 0:
            sent[first - 1][4 * QUARTER :, :] = pack_codes(codes)


def partial_sums(scale, owner, place, act, act_other, cot, cot_other):
    own = jax.ShapeDtypeStruct((4 * QUARTER, HALF), F32)
    sent = jax.ShapeDtypeStruct((4 * QUARTER + TAIL, HALF), I16)
    return pl.pallas_call(
        functools.partial(partial_kernel, scale),
        out_shape=[own, sent, sent, sent],
        in_specs=[SMEM, SMEM, VMEM, VMEM, VMEM, VMEM],
        out_specs=[VMEM] * 4,
        scratch_shapes=[pltpu.VMEM((2, QUARTER, 2 * QUARTER), BF16)],
        compiler_params=params(16),
        cost_estimate=cost(2 * 512 * 512 * 4096, 13 * 2**20),
        name="partial_sums",
    )(owner, place, act, act_other, cot, cot_other)


def middle_kernel(own, first, second, third, after, *outs):
    arrived = (first, second, third)
    scales = [unpack_scales(a[4 * QUARTER :, :]) for a in arrived]
    for position in range(4):
        where = slice(position * QUARTER, (position + 1) * QUARTER)
        total = own[where, :]
        for a, s in zip(arrived, scales):
            total = total + unpack(a[where, :], s[position : position + 1, :])
        if position == 0:
            outs[0][...] = total
        else:
            fixed, code = pack(total)
            outs[position][:QUARTER, :] = fixed
            outs[position][QUARTER:, :] = pack_codes([code])


def middle_sums(arrived, after):
    own = jax.ShapeDtypeStruct((QUARTER, HALF), F32)
    sent = jax.ShapeDtypeStruct((QUARTER + TAIL, HALF), I16)
    return pl.pallas_call(
        middle_kernel,
        out_shape=[own, sent, sent, sent],
        in_specs=[VMEM] * 4 + [ANY],
        out_specs=[VMEM] * 4,
        compiler_params=params(16),
        cost_estimate=cost(2**20, 8 * 2**20),
        name="middle_sums",
    )(*arrived, after)


def last_kernel(own, first, second, third, out):
    total = own[...]
    for a in (first, second, third):
        total = total + unpack(a[:QUARTER, :], unpack_scales(a[QUARTER:, :])[0:1, :])
    fixed, code = pack(total)
    out[:QUARTER, :] = fixed
    out[QUARTER:, :] = pack_codes([code])


def last_sums(arrived):
    return pl.pallas_call(
        last_kernel,
        out_shape=jax.ShapeDtypeStruct((QUARTER + TAIL, HALF), I16),
        in_specs=[VMEM] * 4,
        out_specs=VMEM,
        compiler_params=params(8),
        cost_estimate=cost(2**20, 2 * 2**20),
        name="last_sums",
    )(*arrived)


COL_TILE = 256


def product(left, right, left_rows, right_cols, times=dot):
    value = times(left[0][left_rows], right[1][right_cols])
    value = value + times(left[1][left_rows], right[0][right_cols])
    return value + times(left[0][left_rows], right[0][right_cols])


def matmul(left, right, store):
    def step(index, carry):
        cols = pl.ds(pl.multiple_of(index * COL_TILE, COL_TILE), COL_TILE)
        store(cols, product(left, right, (slice(None), slice(None)), (slice(None), cols)))
        return carry

    lax.fori_loop(0, BS // COL_TILE, step, 0)


def split_into(target):
    def store(cols, value):
        target[0][:, cols], target[1][:, cols] = split(value)

    return store


def split_block(source, target):
    def step(index, carry):
        at = pl.ds(pl.multiple_of(index * 128, 128), 128)
        target[0][at, :], target[1][at, :] = split(source[at, :])
        return carry

    lax.fori_loop(0, BS // 128, step, 0)


def fifth_kernel(root, after, high, low, root_high, root_low, power_high, power_low):
    x, out, power = (root_high, root_low), (high, low), (power_high, power_low)
    split_block(root, x)
    matmul(x, x, split_into(out))
    matmul(out, out, split_into(power))
    matmul(power, x, split_into(out))


def fifth_power(root, after):
    block = jax.ShapeDtypeStruct((BS, BS), BF16)
    return pl.pallas_call(
        fifth_kernel,
        out_shape=[block, block],
        in_specs=[VMEM, ANY],
        out_specs=[VMEM, VMEM],
        scratch_shapes=[pltpu.VMEM((BS, BS), BF16)] * 4,
        compiler_params=params(24),
        cost_estimate=cost(9 * 2 * BS**3, 8 * 2**20),
        name="fifth_power",
    )(root, after)


def update_rows_at(side, group):
    return pl.ds(pl.multiple_of(side * (BS // 2) + group * SUB, SUB), SUB)


def newton_kernel(place, *refs):
    newton_body(place, refs[0:5], refs[5:10], *refs[10:])


def newton_body(place, pieces, other, stat_in, root_in, first_high, first_low,
                  stat_out, a_high, a_low, s_high, s_low, x, taken, left_out,
                  g_high, g_low, b_high, b_low, c_high, c_low, f, sems):
    core, group = place[2], place[3]
    grad, stat = (g_high, g_low), (s_high, s_low)
    a, b, c = (a_high, a_low), (b_high, b_low), (c_high, c_low)
    everything = (slice(None), slice(None))
    stat_copy = pltpu.make_async_copy(stat_in, f, sems.at[0])
    root_copy = pltpu.make_async_copy(root_in, x, sems.at[1])
    stat_copy.start()
    root_copy.start()

    for source, half in ((pieces, core), (other, 1 - core)):
        along_cols = pl.ds(pl.multiple_of(half * HALF, HALF), HALF)
        whole, before, behind, top, bottom = source
        for shift, size, fixed, tail, tail_row in (
            (0, QUARTER, whole, whole, QUARTER),
            (3, QUARTER, before, before, QUARTER),
            (1, QUARTER, behind, behind, QUARTER),
            (2, SUB, top, bottom, SUB),
            (2, SUB, bottom, bottom, SUB),
        ):
            first = (group + shift) % 4 * QUARTER + (SUB if fixed is bottom else 0)
            along_rows = pl.ds(pl.multiple_of(first, SUB), size)
            value = unpack(fixed[:size, :], unpack_scales(tail[tail_row:, :])[0:1, :])

            @pl.when(core == 0)
            def _():
                g_high[along_rows, along_cols], g_low[along_rows, along_cols] = split(value)

            @pl.when(core == 1)
            def _():
                turned = value.T
                g_high[along_cols, along_rows], g_low[along_cols, along_rows] = split(turned)

    stat_copy.wait()
    lower = BS // 2
    for first_row, first_col in ((0, 0), (0, lower), (lower, lower)):
        rows = slice(first_row, first_row + lower)
        for col in range(first_col, first_col + lower, COL_TILE):
            cols = slice(col, col + COL_TILE)
            value = product(grad, grad, (rows, slice(None)), (cols, slice(None)), dot_nt)
            value = STAT_DECAY * f[rows, cols] + (1.0 - STAT_DECAY) / BS * value
            f[rows, cols] = value
            s_high[rows, cols], s_low[rows, cols] = split(value)
            if first_row != first_col:
                value = value.T
                f[cols, rows] = value
                s_high[cols, rows], s_low[cols, rows] = split(value)
    stat_copy = pltpu.make_async_copy(f, stat_out, sems.at[2])
    stat_copy.start()
    root_copy.wait()

    def store_first(cols, value):
        new = (5.0 * x[:, cols] - value) * 0.25
        x[:, cols] = new
        b_high[:, cols], b_low[:, cols] = split(new)

    matmul((first_high, first_low), stat, store_first)
    matmul(b, b, split_into(a))
    matmul(a, a, split_into(c))
    matmul(c, b, split_into(a))

    for side in range(2):
        for source, target in zip(a, b):
            target[side * SUB : (side + 1) * SUB, :] = source[update_rows_at(side, group), :]
    top = slice(0, 2 * SUB)
    for col in range(0, BS, COL_TILE):
        cols = slice(col, col + COL_TILE)
        value = product(b, stat, (top, slice(None)), (slice(None), cols))
        for side in range(2):
            part = slice(side * SUB, (side + 1) * SUB)
            new = (5.0 * x[update_rows_at(side, group), cols] - value[part]) * 0.25
            taken[part, cols] = new
            c_high[part, cols], c_low[part, cols] = split(new)

    @pl.when(core == 0)
    def _():
        for col in range(0, BS, COL_TILE):
            cols = slice(col, col + COL_TILE)
            left_out[:, cols] = product(c, grad, (top, slice(None)), (slice(None), cols))

    stat_copy.wait()


def newton(place, pieces, other, stat, root, first):
    block = jax.ShapeDtypeStruct((BS, BS), F32)
    part = jax.ShapeDtypeStruct((BS, BS), BF16)
    strip = jax.ShapeDtypeStruct((2 * SUB, BS), F32)
    half = pltpu.VMEM((BS, BS), BF16)
    return pl.pallas_call(
        newton_kernel,
        out_shape=[block, part, part, part, part, block, strip, strip],
        in_specs=[SMEM] + [VMEM] * 10 + [HBM, HBM, VMEM, VMEM],
        out_specs=[HBM] + [VMEM] * 7,
        scratch_shapes=[half] * 6 + [pltpu.VMEM((BS, BS), F32), pltpu.SemaphoreType.DMA((3,))],
        compiler_params=params(26),
        cost_estimate=cost(16 * 2 * BS**3, 24 * 2**20),
        name="newton",
    )(place, *pieces, *other, stat, root, *first)


def rest_kernel(place, a_high, a_low, s_high, s_low, x, taken, root_out, r_high, r_low,
                l_high, l_low, full, sems):
    group = place[3]
    left, stat = (l_high, l_low), (s_high, s_low)
    others = []
    for side in range(2):
        for shift in range(1, 4):
            others.append(update_rows_at(side, (group + shift) % 4))
    for index, rows in enumerate(others):
        for source, target in ((a_high, l_high), (a_low, l_low)):
            target[index * SUB : (index + 1) * SUB, :] = source[rows, :]

    def step(index, carry):
        cols = pl.ds(pl.multiple_of(index * COL_TILE, COL_TILE), COL_TILE)
        value = product(left, stat, (slice(None), slice(None)), (slice(None), cols))
        for strip, rows in enumerate(others):
            new = (5.0 * x[rows, cols] - value[strip * SUB : (strip + 1) * SUB]) * 0.25
            full[rows, cols] = new
            r_high[rows, cols], r_low[rows, cols] = split(new)
        for side in range(2):
            rows, new = update_rows_at(side, group), taken[side * SUB : (side + 1) * SUB, cols]
            full[rows, cols] = new
            r_high[rows, cols], r_low[rows, cols] = split(new)
        pltpu.make_async_copy(full.at[:, cols], root_out.at[:, cols], sems.at[index]).start()
        return carry

    lax.fori_loop(0, BS // COL_TILE, step, 0)
    for index in range(BS // COL_TILE):
        cols = slice(index * COL_TILE, (index + 1) * COL_TILE)
        pltpu.make_async_copy(full.at[:, cols], root_out.at[:, cols], sems.at[index]).wait()


def rest_of_root(place, fifth, stat, x, taken):
    part = jax.ShapeDtypeStruct((BS, BS), BF16)
    strip = pltpu.VMEM((6 * SUB, BS), BF16)
    return pl.pallas_call(
        rest_kernel,
        out_shape=[jax.ShapeDtypeStruct((BS, BS), F32), part, part],
        in_specs=[SMEM] + [VMEM] * 6,
        out_specs=[HBM, VMEM, VMEM],
        scratch_shapes=[strip, strip, pltpu.VMEM((BS, BS), F32), pltpu.SemaphoreType.DMA((4,))],
        compiler_params=params(20),
        cost_estimate=cost(3 * 2 * 6 * SUB * BS**2, 4 * 2**20),
        name="rest_of_root",
    )(place, *fifth, *stat, x, taken)


def update_kernel(place, left, r_high, r_low, for_left, for_right, l_high, l_low):
    @pl.when(place[2] == 1)
    def _():
        l_high[...], l_low[...] = split(left[...])
        for col in range(0, BS, COL_TILE):
            cols = slice(col, col + COL_TILE)
            value = product((l_high, l_low), (r_high, r_low), (slice(None), slice(None)), (slice(None), cols))
            value = value.astype(BF16)
            for_left[:, cols] = value[:SUB]
            for_right[:, cols] = value[SUB:]


def update_rows(place, left, root):
    strip = jax.ShapeDtypeStruct((SUB, BS), BF16)
    return pl.pallas_call(
        update_kernel,
        out_shape=[strip, strip],
        in_specs=[SMEM, VMEM, VMEM, VMEM],
        out_specs=[VMEM, VMEM],
        scratch_shapes=[pltpu.VMEM((2 * SUB, BS), BF16)] * 2,
        compiler_params=params(16),
        cost_estimate=cost(3 * 2 * 2 * SUB * BS * BS, 6 * 2**20),
        name="update_rows",
    )(place, left, *root)


def swap(value):
    return lax.ppermute(value, "dp", [(i, i ^ 1) for i in range(32)])


def along(value, step, y_core):
    pairs = []
    for source in range(32):
        z, y, core = source // 8, source // 2 % 4, source % 2
        if core == y_core:
            y = (y + step) % 4
        else:
            z = (z + step) % 4
        pairs.append((source, (z * 4 + y) * 2 + core))
    return lax.ppermute(value, "dp", pairs)


def body(activations, cotangent, owner_table, statistics, warm_roots):
    dp, group = lax.axis_index("dp"), lax.axis_index("group")
    core, y, z = dp % 2, dp // 2 % 4, dp // 8
    place = jnp.stack([z, y, core, group]).astype(jnp.int32)
    scale = 1.0 / math.sqrt(activations.shape[0] * lax.axis_size("dp"))

    sent, cot = fetch(place, activations, cotangent)
    act_other, cot_other = swap(sent), swap(cot)
    out = partial_sums(scale, owner_table, place, activations, act_other, cot, cot_other)
    fifth = fifth_power(warm_roots[0], out[0])

    out = [out[0]] + [along(out[step], step, 0) for step in (2, 1, 3)]
    out = middle_sums(out, fifth[0])
    out = [out[0]] + [along(out[step], step, 1) for step in (2, 1, 3)]
    piece = last_sums(out)

    def around(value, step):
        return lax.ppermute(value, "group", [(i, (i + step) % 4) for i in range(4)])

    before, behind = around(piece, 1), around(piece, -1)
    pieces = [piece, before, behind, around(before[:SUB], 1), around(behind[SUB:], -1)]
    other = [swap(p) for p in pieces]

    outs = newton(place, pieces, other, statistics[0], warm_roots[0], fifth)
    statistic, last_fifth, stat, x, taken, left = outs[0], outs[1:3], outs[3:5], outs[5], outs[6], outs[7]
    left = lax.ppermute(left, "dp", [(2 * k, 2 * k + 1) for k in range(16)])
    root, *root_parts = rest_of_root(place, last_fifth, stat, x, taken)
    for_left, for_right = update_rows(place, left, root_parts)
    back = lax.ppermute(for_left, "dp", [(2 * k + 1, 2 * k) for k in range(16)])
    update = jnp.where(core == 0, back, for_right)
    return (statistic[None], root[None], update[None])


def solution(mesh):
    in_specs = (P("dp", None), P("dp", None), P(), P("dp", None, None), P("dp", None, None))
    out_specs = (P("dp", None, None), P("dp", None, None), P("dp", "group", None))
    return jax.shard_map(body, mesh=mesh, in_specs=in_specs, out_specs=out_specs, check_vma=False)
```

```python
import functools
import math

import jax
import jax.numpy as jnp
from jax import lax
from jax.experimental import pallas as pl
from jax.experimental.pallas import tpu as pltpu
from jax.sharding import PartitionSpec as P

ITERS = 2
STAT_DECAY = 0.95

BF16 = jnp.bfloat16
F8 = jnp.float8_e4m3fn
F32 = jnp.float32
I16 = jnp.int16
VMEM = pl.BlockSpec(memory_space=pltpu.VMEM)
SMEM = pl.BlockSpec(memory_space=pltpu.SMEM)
HBM = pl.BlockSpec(memory_space=pltpu.HBM)
ANY = pl.BlockSpec(memory_space=pl.ANY)

BS = 1024
QUARTER = BS // 4
HALF = BS // 2
SUB = QUARTER // 2
TAIL = 16
STEPS = 128.0
TOP = 32767.0


def params(mib):
    return pltpu.CompilerParams(vmem_limit_bytes=mib * 2**20)


def cost(flops, bytes_accessed):
    return pl.CostEstimate(flops=flops, bytes_accessed=bytes_accessed, transcendentals=0)


def dot(a, b):
    return jnp.dot(a, b, preferred_element_type=F32)


def dot_nt(a, b):
    return lax.dot_general(a, b, (((1,), (1,)), ((), ())), preferred_element_type=F32)


def split(value):
    high = value.astype(BF16)
    return high, (value - high.astype(F32)).astype(BF16)


def pack(value):
    level = jnp.maximum(jnp.max(jnp.abs(value), axis=0, keepdims=True), 1e-32)
    code = jnp.floor(jnp.log2(level) * STEPS) + 2.0
    fixed = jnp.round(value * (TOP * jnp.exp2(code * (-1.0 / STEPS))))
    return fixed.astype(jnp.int32).astype(I16), code


def pack_codes(codes):
    row = lax.broadcasted_iota(jnp.int32, (TAIL, codes[0].shape[1]), 0)
    out = jnp.zeros((TAIL, codes[0].shape[1]), F32)
    for index, code in enumerate(codes):
        out = jnp.where(row == index, code, out)
    return out.astype(jnp.int32).astype(I16)


def unpack_scales(tail):
    return jnp.exp2(tail.astype(jnp.int32).astype(F32) * (1.0 / STEPS)) * (1.0 / TOP)


def unpack(fixed, scale):
    return fixed.astype(jnp.int32).astype(F32) * scale


def fetch_kernel(place, act, cot, kept, sent, cot_out, sems):
    core, group = place[2], place[3]
    copies = []
    for half, target in ((1 - core, sent), (core, kept)):
        for block in range(8):
            source = act.at[:, pl.ds(pl.multiple_of(block * BS + half * HALF, HALF), HALF)]
            copies.append((source, target.at[:, block * HALF : (block + 1) * HALF]))
    for block in range(2):
        source = cot.at[:, pl.ds(pl.multiple_of(block * BS + group * QUARTER, QUARTER), QUARTER)]
        copies.append((source, cot_out.at[:, block * QUARTER : (block + 1) * QUARTER]))
    copies = [pltpu.make_async_copy(s, t, sems.at[i]) for i, (s, t) in enumerate(copies)]
    for copy in copies:
        copy.start()
    for copy in copies:
        copy.wait()


def fetch(place, act, cot):
    half = jax.ShapeDtypeStruct((act.shape[0], act.shape[1] // 2), BF16)
    return pl.pallas_call(
        fetch_kernel,
        out_shape=[half, half, jax.ShapeDtypeStruct((cot.shape[0], 2 * QUARTER), BF16)],
        in_specs=[SMEM, HBM, HBM],
        out_specs=[VMEM] * 3,
        scratch_shapes=[pltpu.SemaphoreType.DMA((18,))],
        compiler_params=params(46),
        cost_estimate=cost(0, 5 * 2**20),
        name="fetch",
    )(place, act, cot)


def partial_kernel(scale, owner, place, act, act_other, cot, cot_other, own, *rest):
    sent, turned = rest[:3], rest[3]
    z, y, core = place[0], place[1], place[2]
    for half in range(2):
        cols = slice(half * QUARTER, (half + 1) * QUARTER)
        turned[half, :, :QUARTER] = cot[:, cols].astype(F32).T.astype(BF16)
        turned[half, :, QUARTER:] = cot_other[:, cols].astype(F32).T.astype(BF16)
    for first in range(4):
        codes = []
        for second in range(4):
            step_y = jnp.where(core == 0, first, second)
            step_z = jnp.where(core == 0, second, first)
            block = owner[(z + step_z) % 4 * 4 + (y + step_y) % 4]
            out_half, in_block = block // 8, block % 8
            cols = pl.ds(pl.multiple_of(in_block * HALF, HALF), HALF)
            rows = turned[out_half]
            term = dot(rows[:, :QUARTER], act[:, cols])
            term = (term + dot(rows[:, QUARTER:], act_other[:, cols])) * scale
            where = slice(second * QUARTER, (second + 1) * QUARTER)
            if first == 0:
                own[where, :] = term
            else:
                fixed, code = pack(term)
                sent[first - 1][where, :] = fixed
                codes.append(code)
        if first > 0:
            sent[first - 1][4 * QUARTER :, :] = pack_codes(codes)


def partial_sums(scale, owner, place, act, act_other, cot, cot_other):
    own = jax.ShapeDtypeStruct((4 * QUARTER, HALF), F32)
    sent = jax.ShapeDtypeStruct((4 * QUARTER + TAIL, HALF), I16)
    return pl.pallas_call(
        functools.partial(partial_kernel, scale),
        out_shape=[own, sent, sent, sent],
        in_specs=[SMEM, SMEM, VMEM, VMEM, VMEM, VMEM],
        out_specs=[VMEM] * 4,
        scratch_shapes=[pltpu.VMEM((2, QUARTER, 2 * QUARTER), BF16)],
        compiler_params=params(16),
        cost_estimate=cost(2 * 512 * 512 * 4096, 13 * 2**20),
        name="partial_sums",
    )(owner, place, act, act_other, cot, cot_other)


def middle_kernel(own, first, second, third, after, *outs):
    arrived = (first, second, third)
    scales = [unpack_scales(a[4 * QUARTER :, :]) for a in arrived]
    for position in range(4):
        where = slice(position * QUARTER, (position + 1) * QUARTER)
        total = own[where, :]
        for a, s in zip(arrived, scales):
            total = total + unpack(a[where, :], s[position : position + 1, :])
        if position == 0:
            outs[0][...] = total
        else:
            fixed, code = pack(total)
            outs[position][:QUARTER, :] = fixed
            outs[position][QUARTER:, :] = pack_codes([code])


def middle_sums(arrived, after):
    own = jax.ShapeDtypeStruct((QUARTER, HALF), F32)
    sent = jax.ShapeDtypeStruct((QUARTER + TAIL, HALF), I16)
    return pl.pallas_call(
        middle_kernel,
        out_shape=[own, sent, sent, sent],
        in_specs=[VMEM] * 4 + [ANY],
        out_specs=[VMEM] * 4,
        compiler_params=params(16),
        cost_estimate=cost(2**20, 8 * 2**20),
        name="middle_sums",
    )(*arrived, after)


def last_kernel(own, first, second, third, after, out):
    total = own[...]
    for a in (first, second, third):
        total = total + unpack(a[:QUARTER, :], unpack_scales(a[QUARTER:, :])[0:1, :])
    fixed, code = pack(total)
    out[:QUARTER, :] = fixed
    out[QUARTER:, :] = pack_codes([code])


def last_sums(arrived, after):
    return pl.pallas_call(
        last_kernel,
        out_shape=jax.ShapeDtypeStruct((QUARTER + TAIL, HALF), I16),
        in_specs=[VMEM] * 4 + [ANY],
        out_specs=VMEM,
        compiler_params=params(8),
        cost_estimate=cost(2**20, 2 * 2**20),
        name="last_sums",
    )(*arrived, after)


COL_TILE = 256


def product(left, right, left_rows, right_cols, times=dot):
    value = times(left[0][left_rows], right[1][right_cols])
    value = value + times(left[1][left_rows], right[0][right_cols])
    return value + times(left[0][left_rows], right[0][right_cols])


def matmul(left, right, store):
    def step(index, carry):
        cols = pl.ds(pl.multiple_of(index * COL_TILE, COL_TILE), COL_TILE)
        store(cols, product(left, right, (slice(None), slice(None)), (slice(None), cols)))
        return carry

    lax.fori_loop(0, BS // COL_TILE, step, 0)


def split_into(target):
    def store(cols, value):
        target[0][:, cols], target[1][:, cols] = split(value)

    return store


WIDE_TILE = 512
FULL_SCALE = 256.0
LOW_SCALE = 256.0


def largest(value):
    return jnp.max(jnp.abs(value), axis=(0, 1), keepdims=True)


def sum_level(left_largest, right_sums):
    return jnp.maximum(left_largest * jnp.max(right_sums, axis=(0, 1), keepdims=True), 1e-30)


def thirds(value, level):
    high = value.astype(BF16)
    wide = high.astype(F32)
    scale = FULL_SCALE / level
    return high, (wide * scale).astype(F8), ((value - wide) * (scale * LOW_SCALE)).astype(F8)


def store_thirds(target, where, value, level):
    for ref, part in zip(target, thirds(value, level)):
        ref[where] = part


def mixed_product(left, right, left_level, right_level, cols):
    small = dot(left[1][...], right[2][:, cols]) + dot(left[2][...], right[1][:, cols])
    small = small * (left_level * (1.0 / FULL_SCALE)) * (right_level * (1.0 / FULL_SCALE / LOW_SCALE))
    return dot(left[0][...], right[0][:, cols]) + small


def mixed_matmul(left, right, left_level, right_level, store):
    def step(index, carry):
        cols = pl.ds(pl.multiple_of(index * WIDE_TILE, WIDE_TILE), WIDE_TILE)
        store(cols, mixed_product(left, right, left_level, right_level, cols))
        return carry

    lax.fori_loop(0, BS // WIDE_TILE, step, 0)


def split_block(source, target):
    def step(index, carry):
        at = pl.ds(pl.multiple_of(index * 128, 128), 128)
        target[0][at, :], target[1][at, :] = split(source[at, :])
        return carry

    lax.fori_loop(0, BS // 128, step, 0)


def fifth_kernel(root, after, high, low, root_high, root_low, power_high, power_low):
    x, out, power = (root_high, root_low), (high, low), (power_high, power_low)
    split_block(root, x)
    matmul(x, x, split_into(out))
    matmul(out, out, split_into(power))
    matmul(power, x, split_into(out))


def fifth_power(root, after):
    block = jax.ShapeDtypeStruct((BS, BS), BF16)
    return pl.pallas_call(
        fifth_kernel,
        out_shape=[block, block],
        in_specs=[VMEM, ANY],
        out_specs=[VMEM, VMEM],
        scratch_shapes=[pltpu.VMEM((BS, BS), BF16)] * 4,
        compiler_params=params(24),
        cost_estimate=cost(9 * 2 * BS**3, 8 * 2**20),
        name="fifth_power",
    )(root, after)


def levels_kernel(high, low, stat, root, after, levels, first_high, first_low):
    def measure(index, carry):
        at = pl.ds(pl.multiple_of(index * 128, 128), 128)
        refs = (high, stat, root)
        return tuple(jnp.maximum(c, largest(r[at, :].astype(F32))) for c, r in zip(carry, refs))

    tops = lax.fori_loop(0, BS // 128, measure, (jnp.zeros((1, 1), F32),) * 3)
    level = jnp.maximum(tops[0], 1e-30) * 1.01

    def convert(index, carry):
        at = pl.ds(pl.multiple_of(index * 128, 128), 128)
        scale = FULL_SCALE / level
        first_high[at, :] = (high[at, :].astype(F32) * scale).astype(F8)
        first_low[at, :] = (low[at, :].astype(F32) * (scale * LOW_SCALE)).astype(F8)
        return carry

    lax.fori_loop(0, BS // 128, convert, 0)
    for row, value in enumerate((level, tops[1], tops[2])):
        levels[row : row + 1, :] = jnp.broadcast_to(value, (1, 128))


def levels_of(fifth, stat, root, after):
    eight = jax.ShapeDtypeStruct((BS, BS), F8)
    return pl.pallas_call(
        levels_kernel,
        out_shape=[jax.ShapeDtypeStruct((8, 128), F32), eight, eight],
        in_specs=[VMEM] * 4 + [ANY],
        out_specs=[VMEM] * 3,
        compiler_params=params(18),
        cost_estimate=cost(2**22, 14 * 2**20),
        name="levels",
    )(*fifth, stat, root, after)


def update_rows_at(side, group):
    return pl.ds(pl.multiple_of(side * (BS // 2) + group * SUB, SUB), SUB)


def newton_kernel(place, *refs):
    newton_body(place, refs[0:5], refs[5:10], *refs[10:])


def newton_body(place, pieces, other, stat_in, root_in, levels, first_0, first_1, first_2,
                stat_out, levels_out, a_0, a_1, a_2, s_0, s_1, s_2, x, taken, left_out,
                g_high, g_low, b_0, b_1, b_2, c_0, c_1, c_2, f, t_high, t_low, sums, tops, sems):
    core, group = place[2], place[3]
    grad, stat, first = (g_high, g_low), (s_0, s_1, s_2), (first_0, first_1, first_2)
    a, b, c = (a_0, a_1, a_2), (b_0, b_1, b_2), (c_0, c_1, c_2)
    stat_copy = pltpu.make_async_copy(stat_in, f, sems.at[0])
    root_copy = pltpu.make_async_copy(root_in, x, sems.at[1])
    stat_copy.start()
    root_copy.start()
    first_level, stat_top, root_top = levels[0:1, 0:1], levels[1:2, 0:1], levels[2:3, 0:1]

    top = jnp.zeros((1, HALF), F32)
    for source in (pieces, other):
        for tail, tail_row in zip(source, (QUARTER, QUARTER, QUARTER, None, SUB)):
            if tail_row is not None:
                top = jnp.maximum(top, unpack_scales(tail[tail_row:, :])[0:1, :] * TOP)
    top = largest(top)
    weight = (1.0 - STAT_DECAY) / BS
    stat_level = jnp.maximum(STAT_DECAY * stat_top + weight * BS * top * top, 1e-30) * 1.01

    for source, half in ((pieces, core), (other, 1 - core)):
        along_cols = pl.ds(pl.multiple_of(half * HALF, HALF), HALF)
        whole, before, behind, top, bottom = source
        for shift, size, fixed, tail, tail_row in (
            (0, QUARTER, whole, whole, QUARTER),
            (3, QUARTER, before, before, QUARTER),
            (1, QUARTER, behind, behind, QUARTER),
            (2, SUB, top, bottom, SUB),
            (2, SUB, bottom, bottom, SUB),
        ):
            start = (group + shift) % 4 * QUARTER + (SUB if fixed is bottom else 0)
            along_rows = pl.ds(pl.multiple_of(start, SUB), size)
            value = unpack(fixed[:size, :], unpack_scales(tail[tail_row:, :])[0:1, :])

            @pl.when(core == 0)
            def _():
                g_high[along_rows, along_cols], g_low[along_rows, along_cols] = split(value)

            @pl.when(core == 1)
            def _():
                turned = value.T
                g_high[along_cols, along_rows], g_low[along_cols, along_rows] = split(turned)

    stat_copy.wait()
    sums[...] = jnp.zeros_like(sums)
    lower = BS // 2
    for first_row, first_col in ((0, 0), (0, lower), (lower, lower)):
        rows = slice(first_row, first_row + lower)
        for col in range(first_col, first_col + lower, COL_TILE):
            cols = slice(col, col + COL_TILE)
            value = product(grad, grad, (rows, slice(None)), (cols, slice(None)), dot_nt)
            value = STAT_DECAY * f[rows, cols] + weight * value
            f[rows, cols] = value
            store_thirds(stat, (rows, cols), value, stat_level)
            sums[0:1, cols] += jnp.sum(jnp.abs(value), axis=0, keepdims=True)
            if first_row != first_col:
                value = value.T
                f[cols, rows] = value
                store_thirds(stat, (cols, rows), value, stat_level)
                sums[0:1, rows] += jnp.sum(jnp.abs(value), axis=0, keepdims=True)
    stat_copy = pltpu.make_async_copy(f, stat_out, sems.at[2])
    stat_copy.start()
    root_copy.wait()

    def note(cols, value):
        size = jnp.abs(value)
        sums[0:1, cols] = jnp.sum(size, axis=0, keepdims=True)
        tops[0:1, cols] = jnp.max(size, axis=0, keepdims=True)

    def noted():
        return jnp.max(tops[0:1, :], axis=(0, 1), keepdims=True), sums[0:1, :]

    root_level = (5.0 * root_top + sum_level(first_level, sums[0:1, :])) * 0.26
    root_level = jnp.maximum(root_level, 1e-30)

    def store_first(cols, value):
        new = (5.0 * x[:, cols] - value) * 0.25
        x[:, cols] = new
        store_thirds(b, (slice(None), cols), new, root_level)
        note(cols, new)

    mixed_matmul(first, stat, first_level, stat_level, store_first)

    def store_into(target, level):
        def store(cols, value):
            store_thirds(target, (slice(None), cols), value, level)
            note(cols, value)

        return store

    root_top, root_sums = noted()
    square_level = sum_level(root_top, root_sums) * 1.01
    mixed_matmul(b, b, root_level, root_level, store_into(a, square_level))
    square_top, square_sums = noted()
    fourth_level = sum_level(square_top, square_sums) * 1.01
    mixed_matmul(a, a, square_level, square_level, store_into(c, fourth_level))
    fourth_top, _ = noted()
    fifth_level = sum_level(fourth_top, root_sums) * 1.01
    mixed_matmul(c, b, fourth_level, root_level, store_into(a, fifth_level))
    levels_out[0:1, :] = jnp.broadcast_to(fifth_level, (1, 128))
    levels_out[1:2, :] = jnp.broadcast_to(stat_level, (1, 128))

    strip = [ref.at[: 2 * SUB, :] for ref in b]
    for side in range(2):
        for source, target in zip(a, strip):
            target[side * SUB : (side + 1) * SUB, :] = source[update_rows_at(side, group), :]
    for col in range(0, BS, COL_TILE):
        cols = slice(col, col + COL_TILE)
        value = mixed_product(strip, stat, fifth_level, stat_level, cols)
        for side in range(2):
            part = slice(side * SUB, (side + 1) * SUB)
            new = (5.0 * x[update_rows_at(side, group), cols] - value[part]) * 0.25
            taken[part, cols] = new
            t_high[part, cols], t_low[part, cols] = split(new)

    @pl.when(core == 0)
    def _():
        for col in range(0, BS, COL_TILE):
            cols = slice(col, col + COL_TILE)
            everything = (slice(None), slice(None))
            left_out[:, cols] = product((t_high, t_low), grad, everything, (slice(None), cols))

    stat_copy.wait()


def newton(place, pieces, other, stat, root, levels, first):
    block = jax.ShapeDtypeStruct((BS, BS), F32)
    parts = [jax.ShapeDtypeStruct((BS, BS), t) for t in (BF16, F8, F8)]
    strip = jax.ShapeDtypeStruct((2 * SUB, BS), F32)
    held = [pltpu.VMEM((BS, BS), t) for t in (BF16, F8, F8)]
    half = pltpu.VMEM((BS, BS), BF16)
    strip_half = pltpu.VMEM((2 * SUB, BS), BF16)
    row = pltpu.VMEM((8, BS), F32)
    return pl.pallas_call(
        newton_kernel,
        out_shape=[block, jax.ShapeDtypeStruct((8, 128), F32), *parts, *parts, block, strip, strip],
        in_specs=[SMEM] + [VMEM] * 10 + [HBM, HBM] + [VMEM] * 4,
        out_specs=[HBM] + [VMEM] * 10,
        scratch_shapes=[half, half, *held, *held, pltpu.VMEM((BS, BS), F32), strip_half, strip_half, row, row]
        + [pltpu.SemaphoreType.DMA((3,))],
        compiler_params=params(27),
        cost_estimate=cost(12 * 2 * BS**3, 24 * 2**20),
        name="newton",
    )(place, *pieces, *other, stat, root, levels, *first)


def rest_kernel(place, levels, a_0, a_1, a_2, s_0, s_1, s_2, x, taken, root_out, r_high, r_low,
                l_0, l_1, l_2, full, sems):
    group = place[3]
    left, stat = (l_0, l_1, l_2), (s_0, s_1, s_2)
    fifth_level, stat_level = levels[0:1, 0:1], levels[1:2, 0:1]
    others = []
    for side in range(2):
        for shift in range(1, 4):
            others.append(update_rows_at(side, (group + shift) % 4))
    for index, rows in enumerate(others):
        for source, target in zip((a_0, a_1, a_2), left):
            target[index * SUB : (index + 1) * SUB, :] = source[rows, :]

    def step(index, carry):
        cols = pl.ds(pl.multiple_of(index * COL_TILE, COL_TILE), COL_TILE)
        value = mixed_product(left, stat, fifth_level, stat_level, cols)
        for strip, rows in enumerate(others):
            new = (5.0 * x[rows, cols] - value[strip * SUB : (strip + 1) * SUB]) * 0.25
            full[rows, cols] = new
            r_high[rows, cols], r_low[rows, cols] = split(new)
        for side in range(2):
            rows, new = update_rows_at(side, group), taken[side * SUB : (side + 1) * SUB, cols]
            full[rows, cols] = new
            r_high[rows, cols], r_low[rows, cols] = split(new)
        pltpu.make_async_copy(full.at[:, cols], root_out.at[:, cols], sems.at[index]).start()
        return carry

    lax.fori_loop(0, BS // COL_TILE, step, 0)
    for index in range(BS // COL_TILE):
        cols = slice(index * COL_TILE, (index + 1) * COL_TILE)
        pltpu.make_async_copy(full.at[:, cols], root_out.at[:, cols], sems.at[index]).wait()


def rest_of_root(place, levels, fifth, stat, x, taken):
    part = jax.ShapeDtypeStruct((BS, BS), BF16)
    strips = [pltpu.VMEM((6 * SUB, BS), t) for t in (BF16, F8, F8)]
    return pl.pallas_call(
        rest_kernel,
        out_shape=[jax.ShapeDtypeStruct((BS, BS), F32), part, part],
        in_specs=[SMEM] + [VMEM] * 9,
        out_specs=[HBM, VMEM, VMEM],
        scratch_shapes=[*strips, pltpu.VMEM((BS, BS), F32), pltpu.SemaphoreType.DMA((4,))],
        compiler_params=params(20),
        cost_estimate=cost(2 * 2 * 6 * SUB * BS**2, 4 * 2**20),
        name="rest_of_root",
    )(place, levels, *fifth, *stat, x, taken)


def update_kernel(place, left, r_high, r_low, for_left, for_right, l_high, l_low):
    @pl.when(place[2] == 1)
    def _():
        l_high[...], l_low[...] = split(left[...])
        for col in range(0, BS, COL_TILE):
            cols = slice(col, col + COL_TILE)
            value = product((l_high, l_low), (r_high, r_low), (slice(None), slice(None)), (slice(None), cols))
            value = value.astype(BF16)
            for_left[:, cols] = value[:SUB]
            for_right[:, cols] = value[SUB:]


def update_rows(place, left, root):
    strip = jax.ShapeDtypeStruct((SUB, BS), BF16)
    return pl.pallas_call(
        update_kernel,
        out_shape=[strip, strip],
        in_specs=[SMEM, VMEM, VMEM, VMEM],
        out_specs=[VMEM, VMEM],
        scratch_shapes=[pltpu.VMEM((2 * SUB, BS), BF16)] * 2,
        compiler_params=params(16),
        cost_estimate=cost(3 * 2 * 2 * SUB * BS * BS, 6 * 2**20),
        name="update_rows",
    )(place, left, *root)


def swap(value):
    return lax.ppermute(value, "dp", [(i, i ^ 1) for i in range(32)])


def along(value, step, y_core):
    pairs = []
    for source in range(32):
        z, y, core = source // 8, source // 2 % 4, source % 2
        if core == y_core:
            y = (y + step) % 4
        else:
            z = (z + step) % 4
        pairs.append((source, (z * 4 + y) * 2 + core))
    return lax.ppermute(value, "dp", pairs)


def body(activations, cotangent, owner_table, statistics, warm_roots):
    dp, group = lax.axis_index("dp"), lax.axis_index("group")
    core, y, z = dp % 2, dp // 2 % 4, dp // 8
    place = jnp.stack([z, y, core, group]).astype(jnp.int32)
    scale = 1.0 / math.sqrt(activations.shape[0] * lax.axis_size("dp"))

    kept, sent, cot = fetch(place, activations, cotangent)
    act_other, cot_other = swap(sent), swap(cot)
    out = partial_sums(scale, owner_table, place, kept, act_other, cot, cot_other)
    fifth = fifth_power(warm_roots[0], out[0])

    out = [out[0]] + [along(out[step], step, 0) for step in (2, 1, 3)]
    out = middle_sums(out, fifth[0])
    levels, *first = levels_of(fifth, statistics[0], warm_roots[0], out[0])
    out = [out[0]] + [along(out[step], step, 1) for step in (2, 1, 3)]
    piece = last_sums(out, levels)

    def around(value, step):
        return lax.ppermute(value, "group", [(i, (i + step) % 4) for i in range(4)])

    before, behind = around(piece, 1), around(piece, -1)
    pieces = [piece, before, behind, around(before[:SUB], 1), around(behind[SUB:], -1)]
    other = [swap(p) for p in pieces]

    outs = newton(place, pieces, other, statistics[0], warm_roots[0], levels, [fifth[0], *first])
    statistic, levels, last_fifth, stat, x, taken, left = outs[0], outs[1], outs[2:5], outs[5:8], *outs[8:]
    left = lax.ppermute(left, "dp", [(2 * k, 2 * k + 1) for k in range(16)])
    root, *root_parts = rest_of_root(place, levels, last_fifth, stat, x, taken)
    for_left, for_right = update_rows(place, left, root_parts)
    back = lax.ppermute(for_left, "dp", [(2 * k + 1, 2 * k) for k in range(16)])
    update = jnp.where(core == 0, back, for_right)
    return (statistic[None], root[None], update[None])


def solution(mesh):
    in_specs = (P("dp", None), P("dp", None), P(), P("dp", None, None), P("dp", None, None))
    out_specs = (P("dp", None, None), P("dp", None, None), P("dp", "group", None))
    return jax.shard_map(body, mesh=mesh, in_specs=in_specs, out_specs=out_specs, check_vma=False)
```

```python
import functools
import math

import jax
import jax.numpy as jnp
from jax import lax
from jax.experimental import pallas as pl
from jax.experimental.pallas import tpu as pltpu
from jax.sharding import PartitionSpec as P

ITERS = 2
STAT_DECAY = 0.95

BF16 = jnp.bfloat16
F8 = jnp.float8_e4m3fn
F32 = jnp.float32
I16 = jnp.int16
VMEM = pl.BlockSpec(memory_space=pltpu.VMEM)
SMEM = pl.BlockSpec(memory_space=pltpu.SMEM)
HBM = pl.BlockSpec(memory_space=pltpu.HBM)
ANY = pl.BlockSpec(memory_space=pl.ANY)

BS = 1024
GRAM_WEIGHT = (1.0 - STAT_DECAY) / BS
QUARTER = BS // 4
HALF = BS // 2
SUB = QUARTER // 2
TAIL = 16
STEPS = 128.0
TOP = 32767.0


def params(mib):
    return pltpu.CompilerParams(vmem_limit_bytes=mib * 2**20)


def cost(flops, bytes_accessed):
    return pl.CostEstimate(flops=flops, bytes_accessed=bytes_accessed, transcendentals=0)


def dot(a, b):
    return jnp.dot(a, b, preferred_element_type=F32)


def dot_nt(a, b):
    return lax.dot_general(a, b, (((1,), (1,)), ((), ())), preferred_element_type=F32)


def split(value):
    high = value.astype(BF16)
    return high, (value - high.astype(F32)).astype(BF16)


def pack(value):
    level = jnp.maximum(jnp.max(jnp.abs(value), axis=0, keepdims=True), 1e-32)
    code = jnp.floor(jnp.log2(level) * STEPS) + 2.0
    fixed = jnp.round(value * (TOP * jnp.exp2(code * (-1.0 / STEPS))))
    return fixed.astype(jnp.int32).astype(I16), code


def pack_codes(codes):
    row = lax.broadcasted_iota(jnp.int32, (TAIL, codes[0].shape[1]), 0)
    out = jnp.zeros((TAIL, codes[0].shape[1]), F32)
    for index, code in enumerate(codes):
        out = jnp.where(row == index, code, out)
    return out.astype(jnp.int32).astype(I16)


def unpack_scales(tail):
    return jnp.exp2(tail.astype(jnp.int32).astype(F32) * (1.0 / STEPS)) * (1.0 / TOP)


def unpack(fixed, scale):
    return fixed.astype(jnp.int32).astype(F32) * scale


def fetch_kernel(place, act, cot, kept, sent, cot_out, sems):
    core, group = place[2], place[3]
    copies = []
    for half, target in ((1 - core, sent), (core, kept)):
        for block in range(8):
            source = act.at[:, pl.ds(pl.multiple_of(block * BS + half * HALF, HALF), HALF)]
            copies.append((source, target.at[:, block * HALF : (block + 1) * HALF]))
    for block in range(2):
        source = cot.at[:, pl.ds(pl.multiple_of(block * BS + group * QUARTER, QUARTER), QUARTER)]
        copies.append((source, cot_out.at[:, block * QUARTER : (block + 1) * QUARTER]))
    copies = [pltpu.make_async_copy(s, t, sems.at[i]) for i, (s, t) in enumerate(copies)]
    for copy in copies:
        copy.start()
    for copy in copies:
        copy.wait()


def fetch(place, act, cot):
    half = jax.ShapeDtypeStruct((act.shape[0], act.shape[1] // 2), BF16)
    return pl.pallas_call(
        fetch_kernel,
        out_shape=[half, half, jax.ShapeDtypeStruct((cot.shape[0], 2 * QUARTER), BF16)],
        in_specs=[SMEM, HBM, HBM],
        out_specs=[VMEM] * 3,
        scratch_shapes=[pltpu.SemaphoreType.DMA((18,))],
        compiler_params=params(46),
        cost_estimate=cost(0, 5 * 2**20),
        name="fetch",
    )(place, act, cot)


def partial_kernel(scale, owner, place, act, act_other, cot, cot_other, own, *rest):
    sent, turned = rest[:3], rest[3]
    z, y, core = place[0], place[1], place[2]
    for half in range(2):
        cols = slice(half * QUARTER, (half + 1) * QUARTER)
        turned[half, :, :QUARTER] = cot[:, cols].astype(F32).T.astype(BF16)
        turned[half, :, QUARTER:] = cot_other[:, cols].astype(F32).T.astype(BF16)
    for first in range(4):
        codes = []
        for second in range(4):
            step_y = jnp.where(core == 0, first, second)
            step_z = jnp.where(core == 0, second, first)
            block = owner[(z + step_z) % 4 * 4 + (y + step_y) % 4]
            out_half, in_block = block // 8, block % 8
            cols = pl.ds(pl.multiple_of(in_block * HALF, HALF), HALF)
            rows = turned[out_half]
            term = dot(rows[:, :QUARTER], act[:, cols])
            term = (term + dot(rows[:, QUARTER:], act_other[:, cols])) * scale
            where = slice(second * QUARTER, (second + 1) * QUARTER)
            if first == 0:
                own[where, :] = term
            else:
                fixed, code = pack(term)
                sent[first - 1][where, :] = fixed
                codes.append(code)
        if first > 0:
            sent[first - 1][4 * QUARTER :, :] = pack_codes(codes)


def partial_sums(scale, owner, place, act, act_other, cot, cot_other):
    own = jax.ShapeDtypeStruct((4 * QUARTER, HALF), F32)
    sent = jax.ShapeDtypeStruct((4 * QUARTER + TAIL, HALF), I16)
    return pl.pallas_call(
        functools.partial(partial_kernel, scale),
        out_shape=[own, sent, sent, sent],
        in_specs=[SMEM, SMEM, VMEM, VMEM, VMEM, VMEM],
        out_specs=[VMEM] * 4,
        scratch_shapes=[pltpu.VMEM((2, QUARTER, 2 * QUARTER), BF16)],
        compiler_params=params(16),
        cost_estimate=cost(2 * 512 * 512 * 4096, 13 * 2**20),
        name="partial_sums",
    )(owner, place, act, act_other, cot, cot_other)


def middle_kernel(own, first, second, third, after, *outs):
    arrived = (first, second, third)
    scales = [unpack_scales(a[4 * QUARTER :, :]) for a in arrived]
    for position in range(4):
        where = slice(position * QUARTER, (position + 1) * QUARTER)
        total = own[where, :]
        for a, s in zip(arrived, scales):
            total = total + unpack(a[where, :], s[position : position + 1, :])
        if position == 0:
            outs[0][...] = total
        else:
            fixed, code = pack(total)
            outs[position][:QUARTER, :] = fixed
            outs[position][QUARTER:, :] = pack_codes([code])


def middle_sums(arrived, after):
    own = jax.ShapeDtypeStruct((QUARTER, HALF), F32)
    sent = jax.ShapeDtypeStruct((QUARTER + TAIL, HALF), I16)
    return pl.pallas_call(
        middle_kernel,
        out_shape=[own, sent, sent, sent],
        in_specs=[VMEM] * 4 + [ANY],
        out_specs=[VMEM] * 4,
        compiler_params=params(16),
        cost_estimate=cost(2**20, 8 * 2**20),
        name="middle_sums",
    )(*arrived, after)


def last_kernel(own, first, second, third, after, out):
    total = own[...]
    for a in (first, second, third):
        total = total + unpack(a[:QUARTER, :], unpack_scales(a[QUARTER:, :])[0:1, :])
    fixed, code = pack(total)
    out[:QUARTER, :] = fixed
    out[QUARTER:, :] = pack_codes([code])


def last_sums(arrived, after):
    return pl.pallas_call(
        last_kernel,
        out_shape=jax.ShapeDtypeStruct((QUARTER + TAIL, HALF), I16),
        in_specs=[VMEM] * 4 + [ANY],
        out_specs=VMEM,
        compiler_params=params(8),
        cost_estimate=cost(2**20, 2 * 2**20),
        name="last_sums",
    )(*arrived, after)


COL_TILE = 256


def product(left, right, left_rows, right_cols, times=dot):
    value = times(left[0][left_rows], right[1][right_cols])
    value = value + times(left[1][left_rows], right[0][right_cols])
    return value + times(left[0][left_rows], right[0][right_cols])


def matmul(left, right, store):
    for col in range(0, BS, COL_TILE):
        cols = slice(col, col + COL_TILE)
        store(cols, product(left, right, (slice(None), slice(None)), (slice(None), cols)))


def split_into(target):
    def store(cols, value):
        target[0][:, cols], target[1][:, cols] = split(value)

    return store


WIDE_TILE = 512
FULL_SCALE = 256.0
LOW_SCALE = 256.0


def largest(value):
    return jnp.max(jnp.abs(value), axis=(0, 1), keepdims=True)


def sum_level(left_largest, right_sums):
    return jnp.maximum(left_largest * jnp.max(right_sums, axis=(0, 1), keepdims=True), 1e-30)


def thirds(value, level):
    high = value.astype(BF16)
    wide = high.astype(F32)
    scale = FULL_SCALE / level
    return high, (wide * scale).astype(F8), ((value - wide) * (scale * LOW_SCALE)).astype(F8)


def store_thirds(target, where, value, level):
    for ref, part in zip(target, thirds(value, level)):
        ref[where] = part


def mixed_product(left, right, left_level, right_level, cols):
    small = dot(left[1][...], right[2][:, cols]) + dot(left[2][...], right[1][:, cols])
    small = small * (left_level * (1.0 / FULL_SCALE)) * (right_level * (1.0 / FULL_SCALE / LOW_SCALE))
    return dot(left[0][...], right[0][:, cols]) + small


def mixed_matmul(left, right, left_level, right_level, store):
    for col in range(0, BS, WIDE_TILE):
        cols = slice(col, col + WIDE_TILE)
        store(cols, mixed_product(left, right, left_level, right_level, cols))


def split_block(source, target):
    def step(index, carry):
        at = pl.ds(pl.multiple_of(index * 128, 128), 128)
        target[0][at, :], target[1][at, :] = split(source[at, :])
        return carry

    lax.fori_loop(0, BS // 128, step, 0)


def fifth_kernel(root, after, high, low, root_high, root_low, power_high, power_low):
    x, out, power = (root_high, root_low), (high, low), (power_high, power_low)
    split_block(root, x)
    matmul(x, x, split_into(out))
    matmul(out, out, split_into(power))
    matmul(power, x, split_into(out))


def fifth_power(root, after):
    block = jax.ShapeDtypeStruct((BS, BS), BF16)
    return pl.pallas_call(
        fifth_kernel,
        out_shape=[block, block],
        in_specs=[VMEM, ANY],
        out_specs=[VMEM, VMEM],
        scratch_shapes=[pltpu.VMEM((BS, BS), BF16)] * 4,
        compiler_params=params(24),
        cost_estimate=cost(9 * 2 * BS**3, 8 * 2**20),
        name="fifth_power",
    )(root, after)


def levels_kernel(high, low, stat, root, after, levels, first_high, first_low):
    def measure(index, carry):
        at = pl.ds(pl.multiple_of(index * 128, 128), 128)
        refs = (high, stat, root)
        return tuple(jnp.maximum(c, largest(r[at, :].astype(F32))) for c, r in zip(carry, refs))

    tops = lax.fori_loop(0, BS // 128, measure, (jnp.zeros((1, 1), F32),) * 3)
    level = jnp.maximum(tops[0], 1e-30) * 1.01

    def convert(index, carry):
        at = pl.ds(pl.multiple_of(index * 128, 128), 128)
        scale = FULL_SCALE / level
        first_high[at, :] = (high[at, :].astype(F32) * scale).astype(F8)
        first_low[at, :] = (low[at, :].astype(F32) * (scale * LOW_SCALE)).astype(F8)
        return carry

    lax.fori_loop(0, BS // 128, convert, 0)
    for row, value in enumerate((level, tops[1], tops[2])):
        levels[row : row + 1, :] = jnp.broadcast_to(value, (1, 128))


def levels_of(fifth, stat, root, after):
    eight = jax.ShapeDtypeStruct((BS, BS), F8)
    return pl.pallas_call(
        levels_kernel,
        out_shape=[jax.ShapeDtypeStruct((8, 128), F32), eight, eight],
        in_specs=[VMEM] * 4 + [ANY],
        out_specs=[VMEM] * 3,
        compiler_params=params(18),
        cost_estimate=cost(2**22, 14 * 2**20),
        name="levels",
    )(*fifth, stat, root, after)


def unpacked(source, group):
    whole, before, behind, top, bottom = source
    for shift, size, fixed, tail, tail_row in (
        (0, QUARTER, whole, whole, QUARTER),
        (3, QUARTER, before, before, QUARTER),
        (1, QUARTER, behind, behind, QUARTER),
        (2, SUB, top, bottom, SUB),
        (2, SUB, bottom, bottom, SUB),
    ):
        start = (group + shift) % 4 * QUARTER + (SUB if fixed is bottom else 0)
        yield start, size, unpack(fixed[:size, :], unpack_scales(tail[tail_row:, :])[0:1, :])


def tiles(first_row, first_col):
    for col in range(first_col, first_col + HALF, COL_TILE):
        yield slice(first_row, first_row + HALF), slice(col, col + COL_TILE)


EVERY_TILE = (*tiles(0, 0), *tiles(0, HALF), *tiles(HALF, HALF))


def own_kernel(place, stat, *refs):
    pieces, (high, low, base) = refs[:5], refs[5:]
    core, group = place[2], place[3]
    own = (high, low)
    every = slice(None)
    for start, size, value in unpacked(pieces, group):

        @pl.when(core == 0)
        def _():
            rows = pl.ds(pl.multiple_of(start, SUB), size)
            high[rows, :], low[rows, :] = split(value)

        @pl.when(core == 1)
        def _():
            rows = pl.ds(pl.multiple_of(start // HALF * HALF, HALF), HALF)
            cols = pl.ds(pl.multiple_of(start % HALF, SUB), size)
            high[rows, cols], low[rows, cols] = split(value.T)

    @pl.when(core == 0)
    def _():
        for rows, cols in EVERY_TILE:
            value = product(own, own, (rows, every), (cols, every), dot_nt)
            base[rows, cols] = STAT_DECAY * stat[rows, cols] + GRAM_WEIGHT * value

    @pl.when(core == 1)
    def _():
        for rows, cols in EVERY_TILE[:4]:
            base[rows, cols] = STAT_DECAY * stat[rows, cols]
        for rows, cols in tiles(HALF, HALF):
            value = 0.0
            for block in (0, HALF):
                left = slice(block, block + HALF)
                right = slice(block + cols.start - HALF, block + cols.stop - HALF)
                value = value + product(own, own, (left, every), (right, every), dot_nt)
            base[rows, cols] = STAT_DECAY * stat[rows, cols] + GRAM_WEIGHT * value


def own_gram(place, stat, pieces):
    half = jax.ShapeDtypeStruct((BS, HALF), BF16)
    return pl.pallas_call(
        own_kernel,
        out_shape=[half, half, jax.ShapeDtypeStruct((BS, BS), F32)],
        in_specs=[SMEM] + [VMEM] * 6,
        out_specs=[VMEM] * 3,
        compiler_params=params(20),
        cost_estimate=cost(3 * BS**3, 2**20),
        name="own_gram",
    )(place, stat, *pieces)


def update_rows_at(side, group):
    return pl.ds(pl.multiple_of(side * (BS // 2) + group * SUB, SUB), SUB)


def newton_kernel(place, other, own_high, own_low, base, root_in, levels, first_0, first_1, first_2,
                  stat_out, levels_out, a_0, a_1, a_2, s_0, s_1, s_2, x, taken, left_out,
                  g_high, g_low, b_0, b_1, b_2, c_0, c_1, c_2, f, t_high, t_low, sums, tops, sems):
    core, group = place[2], place[3]
    grad, stat, first = (g_high, g_low), (s_0, s_1, s_2), (first_0, first_1, first_2)
    a, b, c = (a_0, a_1, a_2), (b_0, b_1, b_2), (c_0, c_1, c_2)
    root_copy = pltpu.make_async_copy(root_in, x, sems.at[0])
    root_copy.start()
    first_level, stat_top, root_top = levels[0:1, 0:1], levels[1:2, 0:1], levels[2:3, 0:1]

    ends = (QUARTER + TAIL) * 3
    pieces = [other.at[i * (QUARTER + TAIL) : (i + 1) * (QUARTER + TAIL), :] for i in range(3)]
    pieces += [other.at[ends : ends + SUB, :], other.at[ends + SUB :, :]]
    every = slice(None)
    bound = jnp.zeros((1, 1), F32)
    for start, size, value in unpacked(pieces, group):
        bound = jnp.maximum(bound, largest(value))

        @pl.when(core == 0)
        def _():
            rows = pl.ds(pl.multiple_of(start, SUB), size)
            g_high[rows, HALF:], g_low[rows, HALF:] = split(value)

        @pl.when(core == 1)
        def _():
            cols = pl.ds(pl.multiple_of(start, SUB), size)
            g_high[:HALF, cols], g_low[:HALF, cols] = split(value.T)

    for target, source in ((g_high, own_high), (g_low, own_low)):

        @pl.when(core == 0)
        def _():
            target[:, :HALF] = source[...]

        @pl.when(core == 1)
        def _():
            for block in (0, HALF):
                target[HALF:, block : block + HALF] = source[block : block + HALF, :]

    bound = jnp.maximum(bound, largest(own_high[...].astype(F32)) * 1.01)
    stat_level = jnp.maximum(STAT_DECAY * stat_top + GRAM_WEIGHT * BS * bound * bound, 1e-30) * 1.01
    sums[...] = jnp.zeros_like(sums)

    def store_stat(rows, cols, value):
        f[rows, cols] = value
        store_thirds(stat, (rows, cols), value, stat_level)
        sums[0:1, cols] += jnp.sum(jnp.abs(value), axis=0, keepdims=True)
        if rows.start < HALF <= cols.start:
            value = value.T
            f[cols, rows] = value
            store_thirds(stat, (cols, rows), value, stat_level)
            sums[0:1, rows] += jnp.sum(jnp.abs(value), axis=0, keepdims=True)

    @pl.when(core == 0)
    def _():
        last = slice(HALF, BS)
        for rows, cols in EVERY_TILE:
            value = product(grad, grad, (rows, last), (cols, last), dot_nt)
            store_stat(rows, cols, base[rows, cols] + GRAM_WEIGHT * value)

    @pl.when(core == 1)
    def _():
        for rows, cols in EVERY_TILE:
            value = base[rows, cols]
            if rows.start == 0:
                value = value + GRAM_WEIGHT * product(grad, grad, (rows, every), (cols, every), dot_nt)
            store_stat(rows, cols, value)

    stat_copy = pltpu.make_async_copy(f, stat_out, sems.at[1])
    stat_copy.start()
    root_copy.wait()

    def note(cols, value):
        size = jnp.abs(value)
        sums[0:1, cols] = jnp.sum(size, axis=0, keepdims=True)
        tops[0:1, cols] = jnp.max(size, axis=0, keepdims=True)

    def noted():
        return jnp.max(tops[0:1, :], axis=(0, 1), keepdims=True), sums[0:1, :]

    root_level = (5.0 * root_top + sum_level(first_level, sums[0:1, :])) * 0.26
    root_level = jnp.maximum(root_level, 1e-30)

    def store_first(cols, value):
        new = (5.0 * x[:, cols] - value) * 0.25
        x[:, cols] = new
        store_thirds(b, (slice(None), cols), new, root_level)
        note(cols, new)

    mixed_matmul(first, stat, first_level, stat_level, store_first)

    def store_into(target, level):
        def store(cols, value):
            store_thirds(target, (slice(None), cols), value, level)
            note(cols, value)

        return store

    root_top, root_sums = noted()
    square_level = sum_level(root_top, root_sums) * 1.01
    mixed_matmul(b, b, root_level, root_level, store_into(a, square_level))
    square_top, square_sums = noted()
    fourth_level = sum_level(square_top, square_sums) * 1.01
    mixed_matmul(a, a, square_level, square_level, store_into(c, fourth_level))
    fourth_top, _ = noted()
    fifth_level = sum_level(fourth_top, root_sums) * 1.01
    mixed_matmul(c, b, fourth_level, root_level, store_into(a, fifth_level))
    levels_out[0:1, :] = jnp.broadcast_to(fifth_level, (1, 128))
    levels_out[1:2, :] = jnp.broadcast_to(stat_level, (1, 128))

    strip = [ref.at[: 2 * SUB, :] for ref in b]
    for side in range(2):
        for source, target in zip(a, strip):
            target[side * SUB : (side + 1) * SUB, :] = source[update_rows_at(side, group), :]
    for col in range(0, BS, COL_TILE):
        cols = slice(col, col + COL_TILE)
        value = mixed_product(strip, stat, fifth_level, stat_level, cols)
        for side in range(2):
            part = slice(side * SUB, (side + 1) * SUB)
            new = (5.0 * x[update_rows_at(side, group), cols] - value[part]) * 0.25
            taken[part, cols] = new
            t_high[part, cols], t_low[part, cols] = split(new)

    @pl.when(core == 0)
    def _():
        for col in range(0, BS, COL_TILE):
            cols = slice(col, col + COL_TILE)
            everything = (slice(None), slice(None))
            left_out[:, cols] = product((t_high, t_low), grad, everything, (slice(None), cols))

    stat_copy.wait()


def newton(place, other, own, root, levels, first):
    block = jax.ShapeDtypeStruct((BS, BS), F32)
    parts = [jax.ShapeDtypeStruct((BS, BS), t) for t in (BF16, F8, F8)]
    strip = jax.ShapeDtypeStruct((2 * SUB, BS), F32)
    held = [pltpu.VMEM((BS, BS), t) for t in (BF16, F8, F8)]
    half = pltpu.VMEM((BS, BS), BF16)
    strip_half = pltpu.VMEM((2 * SUB, BS), BF16)
    row = pltpu.VMEM((8, BS), F32)
    return pl.pallas_call(
        newton_kernel,
        out_shape=[block, jax.ShapeDtypeStruct((8, 128), F32), *parts, *parts, block, strip, strip],
        in_specs=[SMEM] + [VMEM] * 4 + [HBM] + [VMEM] * 4,
        out_specs=[HBM] + [VMEM] * 10,
        scratch_shapes=[half, half, *held, *held, pltpu.VMEM((BS, BS), F32), strip_half, strip_half, row, row]
        + [pltpu.SemaphoreType.DMA((2,))],
        compiler_params=params(27),
        cost_estimate=cost(12 * 2 * BS**3, 24 * 2**20),
        name="newton",
    )(place, other, *own, root, levels, *first)


def rest_kernel(place, levels, a_0, a_1, a_2, s_0, s_1, s_2, x, taken, root_out, r_high, r_low,
                l_0, l_1, l_2, full, sems):
    group = place[3]
    left, stat = (l_0, l_1, l_2), (s_0, s_1, s_2)
    fifth_level, stat_level = levels[0:1, 0:1], levels[1:2, 0:1]
    others = []
    for side in range(2):
        for shift in range(1, 4):
            others.append(update_rows_at(side, (group + shift) % 4))
    for index, rows in enumerate(others):
        for source, target in zip((a_0, a_1, a_2), left):
            target[index * SUB : (index + 1) * SUB, :] = source[rows, :]

    copies = []
    for index in range(BS // COL_TILE):
        cols = slice(index * COL_TILE, (index + 1) * COL_TILE)
        value = mixed_product(left, stat, fifth_level, stat_level, cols)
        for strip, rows in enumerate(others):
            new = (5.0 * x[rows, cols] - value[strip * SUB : (strip + 1) * SUB]) * 0.25
            full[rows, cols] = new
            r_high[rows, cols], r_low[rows, cols] = split(new)
        for side in range(2):
            rows, new = update_rows_at(side, group), taken[side * SUB : (side + 1) * SUB, cols]
            full[rows, cols] = new
            r_high[rows, cols], r_low[rows, cols] = split(new)
        copies.append(pltpu.make_async_copy(full.at[:, cols], root_out.at[:, cols], sems.at[index]))
        copies[-1].start()
    for copy in copies:
        copy.wait()


def rest_of_root(place, levels, fifth, stat, x, taken):
    part = jax.ShapeDtypeStruct((BS, BS), BF16)
    strips = [pltpu.VMEM((6 * SUB, BS), t) for t in (BF16, F8, F8)]
    return pl.pallas_call(
        rest_kernel,
        out_shape=[jax.ShapeDtypeStruct((BS, BS), F32), part, part],
        in_specs=[SMEM] + [VMEM] * 9,
        out_specs=[HBM, VMEM, VMEM],
        scratch_shapes=[*strips, pltpu.VMEM((BS, BS), F32), pltpu.SemaphoreType.DMA((4,))],
        compiler_params=params(20),
        cost_estimate=cost(2 * 2 * 6 * SUB * BS**2, 4 * 2**20),
        name="rest_of_root",
    )(place, levels, *fifth, *stat, x, taken)


def update_kernel(place, left, r_high, r_low, for_left, for_right, l_high, l_low):
    @pl.when(place[2] == 1)
    def _():
        l_high[...], l_low[...] = split(left[...])
        for col in range(0, BS, COL_TILE):
            cols = slice(col, col + COL_TILE)
            value = product((l_high, l_low), (r_high, r_low), (slice(None), slice(None)), (slice(None), cols))
            value = value.astype(BF16)
            for_left[:, cols] = value[:SUB]
            for_right[:, cols] = value[SUB:]


def update_rows(place, left, root):
    strip = jax.ShapeDtypeStruct((SUB, BS), BF16)
    return pl.pallas_call(
        update_kernel,
        out_shape=[strip, strip],
        in_specs=[SMEM, VMEM, VMEM, VMEM],
        out_specs=[VMEM, VMEM],
        scratch_shapes=[pltpu.VMEM((2 * SUB, BS), BF16)] * 2,
        compiler_params=params(16),
        cost_estimate=cost(3 * 2 * 2 * SUB * BS * BS, 6 * 2**20),
        name="update_rows",
    )(place, left, *root)


def swap(value):
    return lax.ppermute(value, "dp", [(i, i ^ 1) for i in range(32)])


def along(value, step, y_core):
    pairs = []
    for source in range(32):
        z, y, core = source // 8, source // 2 % 4, source % 2
        if core == y_core:
            y = (y + step) % 4
        else:
            z = (z + step) % 4
        pairs.append((source, (z * 4 + y) * 2 + core))
    return lax.ppermute(value, "dp", pairs)


def body(activations, cotangent, owner_table, statistics, warm_roots):
    dp, group = lax.axis_index("dp"), lax.axis_index("group")
    core, y, z = dp % 2, dp // 2 % 4, dp // 8
    place = jnp.stack([z, y, core, group]).astype(jnp.int32)
    scale = 1.0 / math.sqrt(activations.shape[0] * lax.axis_size("dp"))

    kept, sent, cot = fetch(place, activations, cotangent)
    act_other, cot_other = swap(sent), swap(cot)
    out = partial_sums(scale, owner_table, place, kept, act_other, cot, cot_other)
    fifth = fifth_power(warm_roots[0], out[0])

    out = [out[0]] + [along(out[step], step, 0) for step in (2, 1, 3)]
    out = middle_sums(out, fifth[0])
    levels, *first = levels_of(fifth, statistics[0], warm_roots[0], out[0])
    out = [out[0]] + [along(out[step], step, 1) for step in (2, 1, 3)]
    piece = last_sums(out, levels)

    def around(value, step):
        return lax.ppermute(value, "group", [(i, (i + step) % 4) for i in range(4)])

    before, behind = around(piece, 1), around(piece, -1)
    pieces = [piece, before, behind, around(before[:SUB], 1), around(behind[SUB:], -1)]
    other = swap(jnp.concatenate(pieces, 0))
    own = own_gram(place, statistics[0], pieces)

    outs = newton(place, other, own, warm_roots[0], levels, [fifth[0], *first])
    statistic, levels, last_fifth, stat, x, taken, left = outs[0], outs[1], outs[2:5], outs[5:8], *outs[8:]
    left = lax.ppermute(left, "dp", [(2 * k, 2 * k + 1) for k in range(16)])
    root, *root_parts = rest_of_root(place, levels, last_fifth, stat, x, taken)
    for_left, for_right = update_rows(place, left, root_parts)
    back = lax.ppermute(for_left, "dp", [(2 * k + 1, 2 * k) for k in range(16)])
    update = jnp.where(core == 0, back, for_right)
    return (statistic[None], root[None], update[None])


def solution(mesh):
    in_specs = (P("dp", None), P("dp", None), P(), P("dp", None, None), P("dp", None, None))
    out_specs = (P("dp", None, None), P("dp", None, None), P("dp", "group", None))
    return jax.shard_map(body, mesh=mesh, in_specs=in_specs, out_specs=out_specs, check_vma=False)
```

```python
import functools
import math

import jax
import jax.numpy as jnp
from jax import lax
from jax.experimental import pallas as pl
from jax.experimental.pallas import tpu as pltpu
from jax.sharding import PartitionSpec as P

ITERS = 2
STAT_DECAY = 0.95

BF16 = jnp.bfloat16
F8 = jnp.float8_e4m3fn
F32 = jnp.float32
I16 = jnp.int16
VMEM = pl.BlockSpec(memory_space=pltpu.VMEM)
SMEM = pl.BlockSpec(memory_space=pltpu.SMEM)
HBM = pl.BlockSpec(memory_space=pltpu.HBM)
ANY = pl.BlockSpec(memory_space=pl.ANY)

BS = 1024
QUARTER = BS // 4
HALF = BS // 2
SUB = QUARTER // 2
TAIL = 16
STEPS = 128.0
TOP = 32767.0


def params(mib):
    return pltpu.CompilerParams(vmem_limit_bytes=mib * 2**20)


def cost(flops, bytes_accessed):
    return pl.CostEstimate(flops=flops, bytes_accessed=bytes_accessed, transcendentals=0)


def dot(a, b):
    return jnp.dot(a, b, preferred_element_type=F32)


def dot_nt(a, b):
    return lax.dot_general(a, b, (((1,), (1,)), ((), ())), preferred_element_type=F32)


def split(value):
    high = value.astype(BF16)
    return high, (value - high.astype(F32)).astype(BF16)


def pack(value):
    level = jnp.maximum(jnp.max(jnp.abs(value), axis=0, keepdims=True), 1e-32)
    code = jnp.floor(jnp.log2(level) * STEPS) + 2.0
    fixed = jnp.round(value * (TOP * jnp.exp2(code * (-1.0 / STEPS))))
    return fixed.astype(jnp.int32).astype(I16), code


def pack_codes(codes):
    row = lax.broadcasted_iota(jnp.int32, (TAIL, codes[0].shape[1]), 0)
    out = jnp.zeros((TAIL, codes[0].shape[1]), F32)
    for index, code in enumerate(codes):
        out = jnp.where(row == index, code, out)
    return out.astype(jnp.int32).astype(I16)


def unpack_scales(tail):
    return jnp.exp2(tail.astype(jnp.int32).astype(F32) * (1.0 / STEPS)) * (1.0 / TOP)


def unpack(fixed, scale):
    return fixed.astype(jnp.int32).astype(F32) * scale


def copy_all(copies, sems):
    copies = [pltpu.make_async_copy(s, t, sems.at[i]) for i, (s, t) in enumerate(copies)]
    for copy in copies:
        copy.start()
    for copy in copies:
        copy.wait()


def half_blocks(act, target, half):
    for block in range(8):
        source = act.at[:, pl.ds(pl.multiple_of(block * BS + half * HALF, HALF), HALF)]
        yield source, target.at[:, block * HALF : (block + 1) * HALF]


def sent_kernel(place, act, sent, sems):
    copy_all(half_blocks(act, sent, 1 - place[2]), sems)


def kept_kernel(place, act, cot, after, kept, cot_out, sems):
    copies = []
    for block in range(2):
        source = cot.at[:, pl.ds(pl.multiple_of(block * BS + place[3] * QUARTER, QUARTER), QUARTER)]
        copies.append((source, cot_out.at[:, block * QUARTER : (block + 1) * QUARTER]))
    copy_all([*copies, *half_blocks(act, kept, place[2])], sems)


def fetch_sent(place, act):
    return pl.pallas_call(
        sent_kernel,
        out_shape=jax.ShapeDtypeStruct((act.shape[0], act.shape[1] // 2), BF16),
        in_specs=[SMEM, HBM],
        out_specs=VMEM,
        scratch_shapes=[pltpu.SemaphoreType.DMA((8,))],
        compiler_params=params(50),
        cost_estimate=cost(0, 4 * 2**20),
        name="fetch_sent",
    )(place, act)


def fetch_kept(place, act, cot, after):
    return pl.pallas_call(
        kept_kernel,
        out_shape=[
            jax.ShapeDtypeStruct((act.shape[0], act.shape[1] // 2), BF16),
            jax.ShapeDtypeStruct((cot.shape[0], 2 * QUARTER), BF16),
        ],
        in_specs=[SMEM, HBM, HBM, ANY],
        out_specs=[VMEM] * 2,
        scratch_shapes=[pltpu.SemaphoreType.DMA((10,))],
        compiler_params=params(46),
        cost_estimate=cost(0, 5 * 2**20),
        name="fetch_kept",
    )(place, act, cot, after)


def partial_kernel(scale, owner, place, act, act_other, cot, cot_other, own, *rest):
    sent, turned = rest[:3], rest[3]
    z, y, core = place[0], place[1], place[2]
    for half in range(2):
        cols = slice(half * QUARTER, (half + 1) * QUARTER)
        turned[half, :, :QUARTER] = cot[:, cols].astype(F32).T.astype(BF16)
        turned[half, :, QUARTER:] = cot_other[:, cols].astype(F32).T.astype(BF16)
    for first in range(4):
        codes = []
        for second in range(4):
            step_y = jnp.where(core == 0, first, second)
            step_z = jnp.where(core == 0, second, first)
            block = owner[(z + step_z) % 4 * 4 + (y + step_y) % 4]
            out_half, in_block = block // 8, block % 8
            cols = pl.ds(pl.multiple_of(in_block * HALF, HALF), HALF)
            rows = turned[out_half]
            term = dot(rows[:, :QUARTER], act[:, cols])
            term = (term + dot(rows[:, QUARTER:], act_other[:, cols])) * scale
            where = slice(second * QUARTER, (second + 1) * QUARTER)
            if first == 0:
                own[where, :] = term
            else:
                fixed, code = pack(term)
                sent[first - 1][where, :] = fixed
                codes.append(code)
        if first > 0:
            sent[first - 1][4 * QUARTER :, :] = pack_codes(codes)


def partial_sums(scale, owner, place, act, act_other, cot, cot_other):
    own = jax.ShapeDtypeStruct((4 * QUARTER, HALF), F32)
    sent = jax.ShapeDtypeStruct((4 * QUARTER + TAIL, HALF), I16)
    return pl.pallas_call(
        functools.partial(partial_kernel, scale),
        out_shape=[own, sent, sent, sent],
        in_specs=[SMEM, SMEM, VMEM, VMEM, VMEM, VMEM],
        out_specs=[VMEM] * 4,
        scratch_shapes=[pltpu.VMEM((2, QUARTER, 2 * QUARTER), BF16)],
        compiler_params=params(16),
        cost_estimate=cost(2 * 512 * 512 * 4096, 13 * 2**20),
        name="partial_sums",
    )(owner, place, act, act_other, cot, cot_other)


def middle_kernel(own, first, second, third, after, *outs):
    arrived = (first, second, third)
    scales = [unpack_scales(a[4 * QUARTER :, :]) for a in arrived]
    for position in range(4):
        where = slice(position * QUARTER, (position + 1) * QUARTER)
        total = own[where, :]
        for a, s in zip(arrived, scales):
            total = total + unpack(a[where, :], s[position : position + 1, :])
        if position == 0:
            outs[0][...] = total
        else:
            fixed, code = pack(total)
            outs[position][:QUARTER, :] = fixed
            outs[position][QUARTER:, :] = pack_codes([code])


def middle_sums(arrived, after):
    own = jax.ShapeDtypeStruct((QUARTER, HALF), F32)
    sent = jax.ShapeDtypeStruct((QUARTER + TAIL, HALF), I16)
    return pl.pallas_call(
        middle_kernel,
        out_shape=[own, sent, sent, sent],
        in_specs=[VMEM] * 4 + [ANY],
        out_specs=[VMEM] * 4,
        compiler_params=params(16),
        cost_estimate=cost(2**20, 8 * 2**20),
        name="middle_sums",
    )(*arrived, after)


def last_kernel(own, first, second, third, after, out):
    total = own[...]
    for a in (first, second, third):
        total = total + unpack(a[:QUARTER, :], unpack_scales(a[QUARTER:, :])[0:1, :])
    fixed, code = pack(total)
    out[:QUARTER, :] = fixed
    out[QUARTER:, :] = pack_codes([code])


def last_sums(arrived, after):
    return pl.pallas_call(
        last_kernel,
        out_shape=jax.ShapeDtypeStruct((QUARTER + TAIL, HALF), I16),
        in_specs=[VMEM] * 4 + [ANY],
        out_specs=VMEM,
        compiler_params=params(8),
        cost_estimate=cost(2**20, 2 * 2**20),
        name="last_sums",
    )(*arrived, after)


COL_TILE = 256


def product(left, right, left_rows, right_cols, times=dot):
    value = times(left[0][left_rows], right[1][right_cols])
    value = value + times(left[1][left_rows], right[0][right_cols])
    return value + times(left[0][left_rows], right[0][right_cols])


def matmul(left, right, store):
    def step(index, carry):
        cols = pl.ds(pl.multiple_of(index * COL_TILE, COL_TILE), COL_TILE)
        store(cols, product(left, right, (slice(None), slice(None)), (slice(None), cols)))
        return carry

    lax.fori_loop(0, BS // COL_TILE, step, 0)


def split_into(target):
    def store(cols, value):
        target[0][:, cols], target[1][:, cols] = split(value)

    return store


WIDE_TILE = 512
FULL_SCALE = 256.0
LOW_SCALE = 256.0


def largest(value):
    return jnp.max(jnp.abs(value), axis=(0, 1), keepdims=True)


def sum_level(left_largest, right_sums):
    return jnp.maximum(left_largest * jnp.max(right_sums, axis=(0, 1), keepdims=True), 1e-30)


def thirds(value, level):
    high = value.astype(BF16)
    wide = high.astype(F32)
    scale = FULL_SCALE / level
    return high, (wide * scale).astype(F8), ((value - wide) * (scale * LOW_SCALE)).astype(F8)


def store_thirds(target, where, value, level):
    for ref, part in zip(target, thirds(value, level)):
        ref[where] = part


def mixed_product(left, right, left_level, right_level, cols):
    small = dot(left[1][...], right[2][:, cols]) + dot(left[2][...], right[1][:, cols])
    small = small * (left_level * (1.0 / FULL_SCALE)) * (right_level * (1.0 / FULL_SCALE / LOW_SCALE))
    return dot(left[0][...], right[0][:, cols]) + small


def mixed_matmul(left, right, left_level, right_level, store):
    def step(index, carry):
        cols = pl.ds(pl.multiple_of(index * WIDE_TILE, WIDE_TILE), WIDE_TILE)
        store(cols, mixed_product(left, right, left_level, right_level, cols))
        return carry

    lax.fori_loop(0, BS // WIDE_TILE, step, 0)


def split_block(source, target):
    def step(index, carry):
        at = pl.ds(pl.multiple_of(index * 128, 128), 128)
        target[0][at, :], target[1][at, :] = split(source[at, :])
        return carry

    lax.fori_loop(0, BS // 128, step, 0)


def fifth_kernel(root, after, high, low, root_high, root_low, power_high, power_low):
    x, out, power = (root_high, root_low), (high, low), (power_high, power_low)
    split_block(root, x)
    matmul(x, x, split_into(out))
    matmul(out, out, split_into(power))
    matmul(power, x, split_into(out))


def fifth_power(root, after):
    block = jax.ShapeDtypeStruct((BS, BS), BF16)
    return pl.pallas_call(
        fifth_kernel,
        out_shape=[block, block],
        in_specs=[VMEM, ANY],
        out_specs=[VMEM, VMEM],
        scratch_shapes=[pltpu.VMEM((BS, BS), BF16)] * 4,
        compiler_params=params(24),
        cost_estimate=cost(9 * 2 * BS**3, 8 * 2**20),
        name="fifth_power",
    )(root, after)


def levels_kernel(high, low, stat, root, after, levels, first_high, first_low):
    def measure(index, carry):
        at = pl.ds(pl.multiple_of(index * 128, 128), 128)
        refs = (high, stat, root)
        return tuple(jnp.maximum(c, largest(r[at, :].astype(F32))) for c, r in zip(carry, refs))

    tops = lax.fori_loop(0, BS // 128, measure, (jnp.zeros((1, 1), F32),) * 3)
    level = jnp.maximum(tops[0], 1e-30) * 1.01

    def convert(index, carry):
        at = pl.ds(pl.multiple_of(index * 128, 128), 128)
        scale = FULL_SCALE / level
        first_high[at, :] = (high[at, :].astype(F32) * scale).astype(F8)
        first_low[at, :] = (low[at, :].astype(F32) * (scale * LOW_SCALE)).astype(F8)
        return carry

    lax.fori_loop(0, BS // 128, convert, 0)
    for row, value in enumerate((level, tops[1], tops[2])):
        levels[row : row + 1, :] = jnp.broadcast_to(value, (1, 128))


def levels_of(fifth, stat, root, after):
    eight = jax.ShapeDtypeStruct((BS, BS), F8)
    return pl.pallas_call(
        levels_kernel,
        out_shape=[jax.ShapeDtypeStruct((8, 128), F32), eight, eight],
        in_specs=[VMEM] * 4 + [ANY],
        out_specs=[VMEM] * 3,
        compiler_params=params(18),
        cost_estimate=cost(2**22, 14 * 2**20),
        name="levels",
    )(*fifth, stat, root, after)


def update_rows_at(side, group):
    return pl.ds(pl.multiple_of(side * (BS // 2) + group * SUB, SUB), SUB)


def newton_kernel(place, *refs):
    newton_body(place, refs[0:5], refs[5:10], *refs[10:])


def newton_body(place, pieces, other, stat_in, root_in, levels, first_0, first_1, first_2,
                stat_out, levels_out, a_0, a_1, a_2, s_0, s_1, s_2, x, taken, left_out,
                g_high, g_low, b_0, b_1, b_2, c_0, c_1, c_2, f, t_high, t_low, sums, tops, sems):
    core, group = place[2], place[3]
    grad, stat, first = (g_high, g_low), (s_0, s_1, s_2), (first_0, first_1, first_2)
    a, b, c = (a_0, a_1, a_2), (b_0, b_1, b_2), (c_0, c_1, c_2)
    stat_copy = pltpu.make_async_copy(stat_in, f, sems.at[0])
    root_copy = pltpu.make_async_copy(root_in, x, sems.at[1])
    stat_copy.start()
    root_copy.start()
    first_level, stat_top, root_top = levels[0:1, 0:1], levels[1:2, 0:1], levels[2:3, 0:1]

    top = jnp.zeros((1, HALF), F32)
    for source in (pieces, other):
        for tail, tail_row in zip(source, (QUARTER, QUARTER, QUARTER, None, SUB)):
            if tail_row is not None:
                top = jnp.maximum(top, unpack_scales(tail[tail_row:, :])[0:1, :] * TOP)
    top = largest(top)
    weight = (1.0 - STAT_DECAY) / BS
    stat_level = jnp.maximum(STAT_DECAY * stat_top + weight * BS * top * top, 1e-30) * 1.01

    for source, half in ((pieces, core), (other, 1 - core)):
        along_cols = pl.ds(pl.multiple_of(half * HALF, HALF), HALF)
        whole, before, behind, top, bottom = source
        for shift, size, fixed, tail, tail_row in (
            (0, QUARTER, whole, whole, QUARTER),
            (3, QUARTER, before, before, QUARTER),
            (1, QUARTER, behind, behind, QUARTER),
            (2, SUB, top, bottom, SUB),
            (2, SUB, bottom, bottom, SUB),
        ):
            start = (group + shift) % 4 * QUARTER + (SUB if fixed is bottom else 0)
            along_rows = pl.ds(pl.multiple_of(start, SUB), size)
            value = unpack(fixed[:size, :], unpack_scales(tail[tail_row:, :])[0:1, :])

            @pl.when(core == 0)
            def _():
                g_high[along_rows, along_cols], g_low[along_rows, along_cols] = split(value)

            @pl.when(core == 1)
            def _():
                turned = value.T
                g_high[along_cols, along_rows], g_low[along_cols, along_rows] = split(turned)

    stat_copy.wait()
    sums[...] = jnp.zeros_like(sums)
    lower = BS // 2
    for first_row, first_col in ((0, 0), (0, lower), (lower, lower)):
        rows = slice(first_row, first_row + lower)
        for col in range(first_col, first_col + lower, COL_TILE):
            cols = slice(col, col + COL_TILE)
            value = product(grad, grad, (rows, slice(None)), (cols, slice(None)), dot_nt)
            value = STAT_DECAY * f[rows, cols] + weight * value
            f[rows, cols] = value
            store_thirds(stat, (rows, cols), value, stat_level)
            sums[0:1, cols] += jnp.sum(jnp.abs(value), axis=0, keepdims=True)
            if first_row != first_col:
                value = value.T
                f[cols, rows] = value
                store_thirds(stat, (cols, rows), value, stat_level)
                sums[0:1, rows] += jnp.sum(jnp.abs(value), axis=0, keepdims=True)
    stat_copy = pltpu.make_async_copy(f, stat_out, sems.at[2])
    stat_copy.start()
    root_copy.wait()

    def note(cols, value):
        size = jnp.abs(value)
        sums[0:1, cols] = jnp.sum(size, axis=0, keepdims=True)
        tops[0:1, cols] = jnp.max(size, axis=0, keepdims=True)

    def noted():
        return jnp.max(tops[0:1, :], axis=(0, 1), keepdims=True), sums[0:1, :]

    root_level = (5.0 * root_top + sum_level(first_level, sums[0:1, :])) * 0.26
    root_level = jnp.maximum(root_level, 1e-30)

    def store_first(cols, value):
        new = (5.0 * x[:, cols] - value) * 0.25
        x[:, cols] = new
        store_thirds(b, (slice(None), cols), new, root_level)
        note(cols, new)

    mixed_matmul(first, stat, first_level, stat_level, store_first)

    def store_into(target, level):
        def store(cols, value):
            store_thirds(target, (slice(None), cols), value, level)
            note(cols, value)

        return store

    root_top, root_sums = noted()
    square_level = sum_level(root_top, root_sums) * 1.01
    mixed_matmul(b, b, root_level, root_level, store_into(a, square_level))
    square_top, square_sums = noted()
    fourth_level = sum_level(square_top, square_sums) * 1.01
    mixed_matmul(a, a, square_level, square_level, store_into(c, fourth_level))
    fourth_top, _ = noted()
    fifth_level = sum_level(fourth_top, root_sums) * 1.01
    mixed_matmul(c, b, fourth_level, root_level, store_into(a, fifth_level))
    levels_out[0:1, :] = jnp.broadcast_to(fifth_level, (1, 128))
    levels_out[1:2, :] = jnp.broadcast_to(stat_level, (1, 128))

    strip = [ref.at[: 2 * SUB, :] for ref in b]
    for side in range(2):
        for source, target in zip(a, strip):
            target[side * SUB : (side + 1) * SUB, :] = source[update_rows_at(side, group), :]
    for col in range(0, BS, COL_TILE):
        cols = slice(col, col + COL_TILE)
        value = mixed_product(strip, stat, fifth_level, stat_level, cols)
        for side in range(2):
            part = slice(side * SUB, (side + 1) * SUB)
            new = (5.0 * x[update_rows_at(side, group), cols] - value[part]) * 0.25
            taken[part, cols] = new
            t_high[part, cols], t_low[part, cols] = split(new)

    @pl.when(core == 0)
    def _():
        for col in range(0, BS, COL_TILE):
            cols = slice(col, col + COL_TILE)
            everything = (slice(None), slice(None))
            left_out[:, cols] = product((t_high, t_low), grad, everything, (slice(None), cols))

    stat_copy.wait()


def newton(place, pieces, other, stat, root, levels, first):
    block = jax.ShapeDtypeStruct((BS, BS), F32)
    parts = [jax.ShapeDtypeStruct((BS, BS), t) for t in (BF16, F8, F8)]
    strip = jax.ShapeDtypeStruct((2 * SUB, BS), F32)
    held = [pltpu.VMEM((BS, BS), t) for t in (BF16, F8, F8)]
    half = pltpu.VMEM((BS, BS), BF16)
    strip_half = pltpu.VMEM((2 * SUB, BS), BF16)
    row = pltpu.VMEM((8, BS), F32)
    return pl.pallas_call(
        newton_kernel,
        out_shape=[block, jax.ShapeDtypeStruct((8, 128), F32), *parts, *parts, block, strip, strip],
        in_specs=[SMEM] + [VMEM] * 10 + [HBM, HBM] + [VMEM] * 4,
        out_specs=[HBM] + [VMEM] * 10,
        scratch_shapes=[half, half, *held, *held, pltpu.VMEM((BS, BS), F32), strip_half, strip_half, row, row]
        + [pltpu.SemaphoreType.DMA((3,))],
        compiler_params=params(27),
        cost_estimate=cost(12 * 2 * BS**3, 24 * 2**20),
        name="newton",
    )(place, *pieces, *other, stat, root, levels, *first)


def rest_kernel(place, levels, a_0, a_1, a_2, s_0, s_1, s_2, x, taken, root_out, r_high, r_low,
                l_0, l_1, l_2, full, sems):
    group = place[3]
    left, stat = (l_0, l_1, l_2), (s_0, s_1, s_2)
    fifth_level, stat_level = levels[0:1, 0:1], levels[1:2, 0:1]
    others = []
    for side in range(2):
        for shift in range(1, 4):
            others.append(update_rows_at(side, (group + shift) % 4))
    for index, rows in enumerate(others):
        for source, target in zip((a_0, a_1, a_2), left):
            target[index * SUB : (index + 1) * SUB, :] = source[rows, :]

    def step(index, carry):
        cols = pl.ds(pl.multiple_of(index * COL_TILE, COL_TILE), COL_TILE)
        value = mixed_product(left, stat, fifth_level, stat_level, cols)
        for strip, rows in enumerate(others):
            new = (5.0 * x[rows, cols] - value[strip * SUB : (strip + 1) * SUB]) * 0.25
            full[rows, cols] = new
            r_high[rows, cols], r_low[rows, cols] = split(new)
        for side in range(2):
            rows, new = update_rows_at(side, group), taken[side * SUB : (side + 1) * SUB, cols]
            full[rows, cols] = new
            r_high[rows, cols], r_low[rows, cols] = split(new)
        pltpu.make_async_copy(full.at[:, cols], root_out.at[:, cols], sems.at[index]).start()
        return carry

    lax.fori_loop(0, BS // COL_TILE, step, 0)
    for index in range(BS // COL_TILE):
        cols = slice(index * COL_TILE, (index + 1) * COL_TILE)
        pltpu.make_async_copy(full.at[:, cols], root_out.at[:, cols], sems.at[index]).wait()


def rest_of_root(place, levels, fifth, stat, x, taken):
    part = jax.ShapeDtypeStruct((BS, BS), BF16)
    strips = [pltpu.VMEM((6 * SUB, BS), t) for t in (BF16, F8, F8)]
    return pl.pallas_call(
        rest_kernel,
        out_shape=[jax.ShapeDtypeStruct((BS, BS), F32), part, part],
        in_specs=[SMEM] + [VMEM] * 9,
        out_specs=[HBM, VMEM, VMEM],
        scratch_shapes=[*strips, pltpu.VMEM((BS, BS), F32), pltpu.SemaphoreType.DMA((4,))],
        compiler_params=params(20),
        cost_estimate=cost(2 * 2 * 6 * SUB * BS**2, 4 * 2**20),
        name="rest_of_root",
    )(place, levels, *fifth, *stat, x, taken)


def update_kernel(place, left, r_high, r_low, for_left, for_right, l_high, l_low):
    @pl.when(place[2] == 1)
    def _():
        l_high[...], l_low[...] = split(left[...])
        for col in range(0, BS, COL_TILE):
            cols = slice(col, col + COL_TILE)
            value = product((l_high, l_low), (r_high, r_low), (slice(None), slice(None)), (slice(None), cols))
            value = value.astype(BF16)
            for_left[:, cols] = value[:SUB]
            for_right[:, cols] = value[SUB:]


def update_rows(place, left, root):
    strip = jax.ShapeDtypeStruct((SUB, BS), BF16)
    return pl.pallas_call(
        update_kernel,
        out_shape=[strip, strip],
        in_specs=[SMEM, VMEM, VMEM, VMEM],
        out_specs=[VMEM, VMEM],
        scratch_shapes=[pltpu.VMEM((2 * SUB, BS), BF16)] * 2,
        compiler_params=params(16),
        cost_estimate=cost(3 * 2 * 2 * SUB * BS * BS, 6 * 2**20),
        name="update_rows",
    )(place, left, *root)


def swap(value):
    return lax.ppermute(value, "dp", [(i, i ^ 1) for i in range(32)])


def along(value, step, y_core):
    pairs = []
    for source in range(32):
        z, y, core = source // 8, source // 2 % 4, source % 2
        if core == y_core:
            y = (y + step) % 4
        else:
            z = (z + step) % 4
        pairs.append((source, (z * 4 + y) * 2 + core))
    return lax.ppermute(value, "dp", pairs)


def body(activations, cotangent, owner_table, statistics, warm_roots):
    dp, group = lax.axis_index("dp"), lax.axis_index("group")
    core, y, z = dp % 2, dp // 2 % 4, dp // 8
    place = jnp.stack([z, y, core, group]).astype(jnp.int32)
    scale = 1.0 / math.sqrt(activations.shape[0] * lax.axis_size("dp"))

    sent = fetch_sent(place, activations)
    kept, cot = fetch_kept(place, activations, cotangent, sent)
    act_other, cot_other = swap(sent), swap(cot)
    out = partial_sums(scale, owner_table, place, kept, act_other, cot, cot_other)
    fifth = fifth_power(warm_roots[0], out[0])

    out = [out[0]] + [along(out[step], step, 0) for step in (2, 1, 3)]
    out = middle_sums(out, fifth[0])
    levels, *first = levels_of(fifth, statistics[0], warm_roots[0], out[0])
    out = [out[0]] + [along(out[step], step, 1) for step in (2, 1, 3)]
    piece = last_sums(out, levels)

    def around(value, step):
        return lax.ppermute(value, "group", [(i, (i + step) % 4) for i in range(4)])

    before, behind = around(piece, 1), around(piece, -1)
    pieces = [piece, before, behind, around(before[:SUB], 1), around(behind[SUB:], -1)]
    other = [swap(p) for p in pieces]

    outs = newton(place, pieces, other, statistics[0], warm_roots[0], levels, [fifth[0], *first])
    statistic, levels, last_fifth, stat, x, taken, left = outs[0], outs[1], outs[2:5], outs[5:8], *outs[8:]
    left = lax.ppermute(left, "dp", [(2 * k, 2 * k + 1) for k in range(16)])
    root, *root_parts = rest_of_root(place, levels, last_fifth, stat, x, taken)
    for_left, for_right = update_rows(place, left, root_parts)
    back = lax.ppermute(for_left, "dp", [(2 * k + 1, 2 * k) for k in range(16)])
    update = jnp.where(core == 0, back, for_right)
    return (statistic[None], root[None], update[None])


def solution(mesh):
    in_specs = (P("dp", None), P("dp", None), P(), P("dp", None, None), P("dp", None, None))
    out_specs = (P("dp", None, None), P("dp", None, None), P("dp", "group", None))
    return jax.shard_map(body, mesh=mesh, in_specs=in_specs, out_specs=out_specs, check_vma=False)
```

```python
import functools
import math

import jax
import jax.numpy as jnp
from jax import lax
from jax.experimental import pallas as pl
from jax.experimental.pallas import tpu as pltpu
from jax.sharding import PartitionSpec as P

ITERS = 2
STAT_DECAY = 0.95

BF16 = jnp.bfloat16
F8 = jnp.float8_e4m3fn
F32 = jnp.float32
I16 = jnp.int16
VMEM = pl.BlockSpec(memory_space=pltpu.VMEM)
SMEM = pl.BlockSpec(memory_space=pltpu.SMEM)
HBM = pl.BlockSpec(memory_space=pltpu.HBM)
ANY = pl.BlockSpec(memory_space=pl.ANY)

BS = 1024
QUARTER = BS // 4
HALF = BS // 2
SUB = QUARTER // 2
TAIL = 16
STEPS = 128.0
TOP = 32767.0


def params(mib):
    return pltpu.CompilerParams(vmem_limit_bytes=mib * 2**20)


def cost(flops, bytes_accessed):
    return pl.CostEstimate(flops=flops, bytes_accessed=bytes_accessed, transcendentals=0)


def dot(a, b):
    return jnp.dot(a, b, preferred_element_type=F32)


def dot_nt(a, b):
    return lax.dot_general(a, b, (((1,), (1,)), ((), ())), preferred_element_type=F32)


def split(value):
    high = value.astype(BF16)
    return high, (value - high.astype(F32)).astype(BF16)


def pack(value):
    level = jnp.maximum(jnp.max(jnp.abs(value), axis=0, keepdims=True), 1e-32)
    code = jnp.floor(jnp.log2(level) * STEPS) + 2.0
    fixed = jnp.round(value * (TOP * jnp.exp2(code * (-1.0 / STEPS))))
    return fixed.astype(jnp.int32).astype(I16), code


def pack_codes(codes):
    row = lax.broadcasted_iota(jnp.int32, (TAIL, codes[0].shape[1]), 0)
    out = jnp.zeros((TAIL, codes[0].shape[1]), F32)
    for index, code in enumerate(codes):
        out = jnp.where(row == index, code, out)
    return out.astype(jnp.int32).astype(I16)


def unpack_scales(tail):
    return jnp.exp2(tail.astype(jnp.int32).astype(F32) * (1.0 / STEPS)) * (1.0 / TOP)


def unpack(fixed, scale):
    return fixed.astype(jnp.int32).astype(F32) * scale


def copy_all(copies, sems):
    copies = [pltpu.make_async_copy(s, t, sems.at[i]) for i, (s, t) in enumerate(copies)]
    for copy in copies:
        copy.start()
    for copy in copies:
        copy.wait()


def half_blocks(act, target, half):
    for block in range(8):
        source = act.at[:, pl.ds(pl.multiple_of(block * BS + half * HALF, HALF), HALF)]
        yield source, target.at[:, block * HALF : (block + 1) * HALF]


def sent_kernel(place, act, sent, sems):
    copy_all(half_blocks(act, sent, 1 - place[2]), sems)


def kept_kernel(place, act, cot, after, kept, cot_out, sems):
    copies = []
    for block in range(2):
        source = cot.at[:, pl.ds(pl.multiple_of(block * BS + place[3] * QUARTER, QUARTER), QUARTER)]
        copies.append((source, cot_out.at[:, block * QUARTER : (block + 1) * QUARTER]))
    copy_all([*copies, *half_blocks(act, kept, place[2])], sems)


def fetch_sent(place, act):
    return pl.pallas_call(
        sent_kernel,
        out_shape=jax.ShapeDtypeStruct((act.shape[0], act.shape[1] // 2), BF16),
        in_specs=[SMEM, HBM],
        out_specs=VMEM,
        scratch_shapes=[pltpu.SemaphoreType.DMA((8,))],
        compiler_params=params(50),
        cost_estimate=cost(0, 4 * 2**20),
        name="fetch_sent",
    )(place, act)


def fetch_kept(place, act, cot, after):
    return pl.pallas_call(
        kept_kernel,
        out_shape=[
            jax.ShapeDtypeStruct((act.shape[0], act.shape[1] // 2), BF16),
            jax.ShapeDtypeStruct((cot.shape[0], 2 * QUARTER), BF16),
        ],
        in_specs=[SMEM, HBM, HBM, ANY],
        out_specs=[VMEM] * 2,
        scratch_shapes=[pltpu.SemaphoreType.DMA((10,))],
        compiler_params=params(46),
        cost_estimate=cost(0, 5 * 2**20),
        name="fetch_kept",
    )(place, act, cot, after)


def partial_kernel(scale, owner, place, act, act_other, cot, cot_other, own, *rest):
    sent, turned = rest[:3], rest[3]
    z, y, core = place[0], place[1], place[2]
    for half in range(2):
        cols = slice(half * QUARTER, (half + 1) * QUARTER)
        turned[half, :, :QUARTER] = cot[:, cols].astype(F32).T.astype(BF16)
        turned[half, :, QUARTER:] = cot_other[:, cols].astype(F32).T.astype(BF16)
    for first in range(4):
        codes = []
        for second in range(4):
            step_y = jnp.where(core == 0, first, second)
            step_z = jnp.where(core == 0, second, first)
            block = owner[(z + step_z) % 4 * 4 + (y + step_y) % 4]
            out_half, in_block = block // 8, block % 8
            cols = pl.ds(pl.multiple_of(in_block * HALF, HALF), HALF)
            rows = turned[out_half]
            term = dot(rows[:, :QUARTER], act[:, cols])
            term = (term + dot(rows[:, QUARTER:], act_other[:, cols])) * scale
            where = slice(second * QUARTER, (second + 1) * QUARTER)
            if first == 0:
                own[where, :] = term
            else:
                fixed, code = pack(term)
                sent[first - 1][where, :] = fixed
                codes.append(code)
        if first > 0:
            sent[first - 1][4 * QUARTER :, :] = pack_codes(codes)


def partial_sums(scale, owner, place, act, act_other, cot, cot_other):
    own = jax.ShapeDtypeStruct((4 * QUARTER, HALF), F32)
    sent = jax.ShapeDtypeStruct((4 * QUARTER + TAIL, HALF), I16)
    return pl.pallas_call(
        functools.partial(partial_kernel, scale),
        out_shape=[own, sent, sent, sent],
        in_specs=[SMEM, SMEM, VMEM, VMEM, VMEM, VMEM],
        out_specs=[VMEM] * 4,
        scratch_shapes=[pltpu.VMEM((2, QUARTER, 2 * QUARTER), BF16)],
        compiler_params=params(16),
        cost_estimate=cost(2 * 512 * 512 * 4096, 13 * 2**20),
        name="partial_sums",
    )(owner, place, act, act_other, cot, cot_other)


def middle_kernel(own, first, second, third, after, *outs):
    arrived = (first, second, third)
    scales = [unpack_scales(a[4 * QUARTER :, :]) for a in arrived]
    for position in range(4):
        where = slice(position * QUARTER, (position + 1) * QUARTER)
        total = own[where, :]
        for a, s in zip(arrived, scales):
            total = total + unpack(a[where, :], s[position : position + 1, :])
        if position == 0:
            outs[0][...] = total
        else:
            fixed, code = pack(total)
            outs[position][:QUARTER, :] = fixed
            outs[position][QUARTER:, :] = pack_codes([code])


def middle_sums(arrived, after):
    own = jax.ShapeDtypeStruct((QUARTER, HALF), F32)
    sent = jax.ShapeDtypeStruct((QUARTER + TAIL, HALF), I16)
    return pl.pallas_call(
        middle_kernel,
        out_shape=[own, sent, sent, sent],
        in_specs=[VMEM] * 4 + [ANY],
        out_specs=[VMEM] * 4,
        compiler_params=params(16),
        cost_estimate=cost(2**20, 8 * 2**20),
        name="middle_sums",
    )(*arrived, after)


def last_kernel(own, first, second, third, after, out):
    total = own[...]
    for a in (first, second, third):
        total = total + unpack(a[:QUARTER, :], unpack_scales(a[QUARTER:, :])[0:1, :])
    fixed, code = pack(total)
    out[:QUARTER, :] = fixed
    out[QUARTER:, :] = pack_codes([code])


def last_sums(arrived, after):
    return pl.pallas_call(
        last_kernel,
        out_shape=jax.ShapeDtypeStruct((QUARTER + TAIL, HALF), I16),
        in_specs=[VMEM] * 4 + [ANY],
        out_specs=VMEM,
        compiler_params=params(8),
        cost_estimate=cost(2**20, 2 * 2**20),
        name="last_sums",
    )(*arrived, after)


COL_TILE = 256


def product(left, right, left_rows, right_cols, times=dot):
    value = times(left[0][left_rows], right[1][right_cols])
    value = value + times(left[1][left_rows], right[0][right_cols])
    return value + times(left[0][left_rows], right[0][right_cols])


def matmul(left, right, store):
    def step(index, carry):
        cols = pl.ds(pl.multiple_of(index * COL_TILE, COL_TILE), COL_TILE)
        store(cols, product(left, right, (slice(None), slice(None)), (slice(None), cols)))
        return carry

    lax.fori_loop(0, BS // COL_TILE, step, 0)


def split_into(target):
    def store(cols, value):
        target[0][:, cols], target[1][:, cols] = split(value)

    return store


WIDE_TILE = 512
FULL_SCALE = 256.0
LOW_SCALE = 256.0


def largest(value):
    return jnp.max(jnp.abs(value), axis=(0, 1), keepdims=True)


def sum_level(left_largest, right_sums):
    return jnp.maximum(left_largest * jnp.max(right_sums, axis=(0, 1), keepdims=True), 1e-30)


def thirds(value, level):
    high = value.astype(BF16)
    wide = high.astype(F32)
    scale = FULL_SCALE / level
    return high, (wide * scale).astype(F8), ((value - wide) * (scale * LOW_SCALE)).astype(F8)


def store_thirds(target, where, value, level):
    for ref, part in zip(target, thirds(value, level)):
        ref[where] = part


def mixed_product(left, right, left_level, right_level, cols):
    small = dot(left[1][...], right[2][:, cols]) + dot(left[2][...], right[1][:, cols])
    small = small * (left_level * (1.0 / FULL_SCALE)) * (right_level * (1.0 / FULL_SCALE / LOW_SCALE))
    return dot(left[0][...], right[0][:, cols]) + small


def mixed_matmul(left, right, left_level, right_level, store):
    def step(index, carry):
        cols = pl.ds(pl.multiple_of(index * WIDE_TILE, WIDE_TILE), WIDE_TILE)
        store(cols, mixed_product(left, right, left_level, right_level, cols))
        return carry

    lax.fori_loop(0, BS // WIDE_TILE, step, 0)


def split_block(source, target):
    def step(index, carry):
        at = pl.ds(pl.multiple_of(index * 128, 128), 128)
        target[0][at, :], target[1][at, :] = split(source[at, :])
        return carry

    lax.fori_loop(0, BS // 128, step, 0)


def fifth_kernel(root, after, high, low, highs, lows):
    def power(index):
        return highs.at[index], lows.at[index]

    def square(index, carry):
        matmul(power(index), power(index), split_into(power(index + 1)))
        return carry

    split_block(root, power(0))
    lax.fori_loop(0, 2, square, 0)
    matmul(power(2), power(0), split_into((high, low)))


def fifth_power(root, after):
    block = jax.ShapeDtypeStruct((BS, BS), BF16)
    return pl.pallas_call(
        fifth_kernel,
        out_shape=[block, block],
        in_specs=[VMEM, ANY],
        out_specs=[VMEM, VMEM],
        scratch_shapes=[pltpu.VMEM((3, BS, BS), BF16)] * 2,
        compiler_params=params(28),
        cost_estimate=cost(9 * 2 * BS**3, 8 * 2**20),
        name="fifth_power",
    )(root, after)


def levels_kernel(high, low, stat, root, after, levels, first_high, first_low):
    def measure(index, carry):
        at = pl.ds(pl.multiple_of(index * 128, 128), 128)
        refs = (high, stat, root)
        return tuple(jnp.maximum(c, largest(r[at, :].astype(F32))) for c, r in zip(carry, refs))

    tops = lax.fori_loop(0, BS // 128, measure, (jnp.zeros((1, 1), F32),) * 3)
    level = jnp.maximum(tops[0], 1e-30) * 1.01

    def convert(index, carry):
        at = pl.ds(pl.multiple_of(index * 128, 128), 128)
        scale = FULL_SCALE / level
        first_high[at, :] = (high[at, :].astype(F32) * scale).astype(F8)
        first_low[at, :] = (low[at, :].astype(F32) * (scale * LOW_SCALE)).astype(F8)
        return carry

    lax.fori_loop(0, BS // 128, convert, 0)
    for row, value in enumerate((level, tops[1], tops[2])):
        levels[row : row + 1, :] = jnp.broadcast_to(value, (1, 128))


def levels_of(fifth, stat, root, after):
    eight = jax.ShapeDtypeStruct((BS, BS), F8)
    return pl.pallas_call(
        levels_kernel,
        out_shape=[jax.ShapeDtypeStruct((8, 128), F32), eight, eight],
        in_specs=[VMEM] * 4 + [ANY],
        out_specs=[VMEM] * 3,
        compiler_params=params(18),
        cost_estimate=cost(2**22, 14 * 2**20),
        name="levels",
    )(*fifth, stat, root, after)


def update_rows_at(side, group):
    return pl.ds(pl.multiple_of(side * (BS // 2) + group * SUB, SUB), SUB)


def newton_kernel(place, *refs):
    newton_body(place, refs[0:5], refs[5:10], *refs[10:])


def newton_body(place, pieces, other, stat_in, root_in, levels, first_0, first_1, first_2,
                stat_out, levels_out, a_0, a_1, a_2, s_0, s_1, s_2, x, taken, left_out,
                g_high, g_low, b_0, b_1, b_2, c_0, c_1, c_2, f, t_high, t_low, sums, tops, sems):
    core, group = place[2], place[3]
    grad, stat, first = (g_high, g_low), (s_0, s_1, s_2), (first_0, first_1, first_2)
    a, b, c = (a_0, a_1, a_2), (b_0, b_1, b_2), (c_0, c_1, c_2)
    stat_copy = pltpu.make_async_copy(stat_in, f, sems.at[0])
    root_copy = pltpu.make_async_copy(root_in, x, sems.at[1])
    stat_copy.start()
    root_copy.start()
    first_level, stat_top, root_top = levels[0:1, 0:1], levels[1:2, 0:1], levels[2:3, 0:1]

    top = jnp.zeros((1, HALF), F32)
    for source in (pieces, other):
        for tail, tail_row in zip(source, (QUARTER, QUARTER, QUARTER, None, SUB)):
            if tail_row is not None:
                top = jnp.maximum(top, unpack_scales(tail[tail_row:, :])[0:1, :] * TOP)
    top = largest(top)
    weight = (1.0 - STAT_DECAY) / BS
    stat_level = jnp.maximum(STAT_DECAY * stat_top + weight * BS * top * top, 1e-30) * 1.01

    for source, half in ((pieces, core), (other, 1 - core)):
        along_cols = pl.ds(pl.multiple_of(half * HALF, HALF), HALF)
        whole, before, behind, top, bottom = source
        for shift, size, fixed, tail, tail_row in (
            (0, QUARTER, whole, whole, QUARTER),
            (3, QUARTER, before, before, QUARTER),
            (1, QUARTER, behind, behind, QUARTER),
            (2, SUB, top, bottom, SUB),
            (2, SUB, bottom, bottom, SUB),
        ):
            start = (group + shift) % 4 * QUARTER + (SUB if fixed is bottom else 0)
            along_rows = pl.ds(pl.multiple_of(start, SUB), size)
            value = unpack(fixed[:size, :], unpack_scales(tail[tail_row:, :])[0:1, :])

            @pl.when(core == 0)
            def _():
                g_high[along_rows, along_cols], g_low[along_rows, along_cols] = split(value)

            @pl.when(core == 1)
            def _():
                turned = value.T
                g_high[along_cols, along_rows], g_low[along_cols, along_rows] = split(turned)

    stat_copy.wait()
    sums[...] = jnp.zeros_like(sums)
    lower = BS // 2
    for first_row, first_col in ((0, 0), (0, lower), (lower, lower)):
        rows = slice(first_row, first_row + lower)
        for col in range(first_col, first_col + lower, COL_TILE):
            cols = slice(col, col + COL_TILE)
            value = product(grad, grad, (rows, slice(None)), (cols, slice(None)), dot_nt)
            value = STAT_DECAY * f[rows, cols] + weight * value
            f[rows, cols] = value
            store_thirds(stat, (rows, cols), value, stat_level)
            sums[0:1, cols] += jnp.sum(jnp.abs(value), axis=0, keepdims=True)
            if first_row != first_col:
                value = value.T
                f[cols, rows] = value
                store_thirds(stat, (cols, rows), value, stat_level)
                sums[0:1, rows] += jnp.sum(jnp.abs(value), axis=0, keepdims=True)
    stat_copy = pltpu.make_async_copy(f, stat_out, sems.at[2])
    stat_copy.start()
    root_copy.wait()

    def note(cols, value):
        size = jnp.abs(value)
        sums[0:1, cols] = jnp.sum(size, axis=0, keepdims=True)
        tops[0:1, cols] = jnp.max(size, axis=0, keepdims=True)

    def noted():
        return jnp.max(tops[0:1, :], axis=(0, 1), keepdims=True), sums[0:1, :]

    root_level = (5.0 * root_top + sum_level(first_level, sums[0:1, :])) * 0.26
    root_level = jnp.maximum(root_level, 1e-30)

    def store_first(cols, value):
        new = (5.0 * x[:, cols] - value) * 0.25
        x[:, cols] = new
        store_thirds(b, (slice(None), cols), new, root_level)
        note(cols, new)

    mixed_matmul(first, stat, first_level, stat_level, store_first)

    def store_into(target, level):
        def store(cols, value):
            store_thirds(target, (slice(None), cols), value, level)
            note(cols, value)

        return store

    root_top, root_sums = noted()
    square_level = sum_level(root_top, root_sums) * 1.01
    mixed_matmul(b, b, root_level, root_level, store_into(a, square_level))
    square_top, square_sums = noted()
    fourth_level = sum_level(square_top, square_sums) * 1.01
    mixed_matmul(a, a, square_level, square_level, store_into(c, fourth_level))
    fourth_top, _ = noted()
    fifth_level = sum_level(fourth_top, root_sums) * 1.01
    mixed_matmul(c, b, fourth_level, root_level, store_into(a, fifth_level))
    levels_out[0:1, :] = jnp.broadcast_to(fifth_level, (1, 128))
    levels_out[1:2, :] = jnp.broadcast_to(stat_level, (1, 128))

    strip = [ref.at[: 2 * SUB, :] for ref in b]
    for side in range(2):
        for source, target in zip(a, strip):
            target[side * SUB : (side + 1) * SUB, :] = source[update_rows_at(side, group), :]
    for col in range(0, BS, COL_TILE):
        cols = slice(col, col + COL_TILE)
        value = mixed_product(strip, stat, fifth_level, stat_level, cols)
        for side in range(2):
            part = slice(side * SUB, (side + 1) * SUB)
            new = (5.0 * x[update_rows_at(side, group), cols] - value[part]) * 0.25
            taken[part, cols] = new
            t_high[part, cols], t_low[part, cols] = split(new)

    @pl.when(core == 0)
    def _():
        for col in range(0, BS, COL_TILE):
            cols = slice(col, col + COL_TILE)
            everything = (slice(None), slice(None))
            left_out[:, cols] = product((t_high, t_low), grad, everything, (slice(None), cols))

    stat_copy.wait()


def newton(place, pieces, other, stat, root, levels, first):
    block = jax.ShapeDtypeStruct((BS, BS), F32)
    parts = [jax.ShapeDtypeStruct((BS, BS), t) for t in (BF16, F8, F8)]
    strip = jax.ShapeDtypeStruct((2 * SUB, BS), F32)
    held = [pltpu.VMEM((BS, BS), t) for t in (BF16, F8, F8)]
    half = pltpu.VMEM((BS, BS), BF16)
    strip_half = pltpu.VMEM((2 * SUB, BS), BF16)
    row = pltpu.VMEM((8, BS), F32)
    return pl.pallas_call(
        newton_kernel,
        out_shape=[block, jax.ShapeDtypeStruct((8, 128), F32), *parts, *parts, block, strip, strip],
        in_specs=[SMEM] + [VMEM] * 10 + [HBM, HBM] + [VMEM] * 4,
        out_specs=[HBM] + [VMEM] * 10,
        scratch_shapes=[half, half, *held, *held, pltpu.VMEM((BS, BS), F32), strip_half, strip_half, row, row]
        + [pltpu.SemaphoreType.DMA((3,))],
        compiler_params=params(27),
        cost_estimate=cost(12 * 2 * BS**3, 24 * 2**20),
        name="newton",
    )(place, *pieces, *other, stat, root, levels, *first)


def rest_kernel(place, levels, a_0, a_1, a_2, s_0, s_1, s_2, x, taken, root_out, r_high, r_low,
                l_0, l_1, l_2, full, sems):
    group = place[3]
    left, stat = (l_0, l_1, l_2), (s_0, s_1, s_2)
    fifth_level, stat_level = levels[0:1, 0:1], levels[1:2, 0:1]
    others = []
    for side in range(2):
        for shift in range(1, 4):
            others.append(update_rows_at(side, (group + shift) % 4))
    for index, rows in enumerate(others):
        for source, target in zip((a_0, a_1, a_2), left):
            target[index * SUB : (index + 1) * SUB, :] = source[rows, :]

    copies = []
    for index in range(BS // COL_TILE):
        cols = slice(index * COL_TILE, (index + 1) * COL_TILE)
        value = mixed_product(left, stat, fifth_level, stat_level, cols)
        for strip, rows in enumerate(others):
            new = (5.0 * x[rows, cols] - value[strip * SUB : (strip + 1) * SUB]) * 0.25
            full[rows, cols] = new
            r_high[rows, cols], r_low[rows, cols] = split(new)
        for side in range(2):
            rows, new = update_rows_at(side, group), taken[side * SUB : (side + 1) * SUB, cols]
            full[rows, cols] = new
            r_high[rows, cols], r_low[rows, cols] = split(new)
        copies.append(pltpu.make_async_copy(full.at[:, cols], root_out.at[:, cols], sems.at[index]))
        copies[-1].start()
    for copy in copies:
        copy.wait()


def rest_of_root(place, levels, fifth, stat, x, taken):
    part = jax.ShapeDtypeStruct((BS, BS), BF16)
    strips = [pltpu.VMEM((6 * SUB, BS), t) for t in (BF16, F8, F8)]
    return pl.pallas_call(
        rest_kernel,
        out_shape=[jax.ShapeDtypeStruct((BS, BS), F32), part, part],
        in_specs=[SMEM] + [VMEM] * 9,
        out_specs=[HBM, VMEM, VMEM],
        scratch_shapes=[*strips, pltpu.VMEM((BS, BS), F32), pltpu.SemaphoreType.DMA((4,))],
        compiler_params=params(20),
        cost_estimate=cost(2 * 2 * 6 * SUB * BS**2, 4 * 2**20),
        name="rest_of_root",
    )(place, levels, *fifth, *stat, x, taken)


def update_kernel(place, left, r_high, r_low, for_left, for_right, l_high, l_low):
    @pl.when(place[2] == 1)
    def _():
        l_high[...], l_low[...] = split(left[...])
        for col in range(0, BS, COL_TILE):
            cols = slice(col, col + COL_TILE)
            value = product((l_high, l_low), (r_high, r_low), (slice(None), slice(None)), (slice(None), cols))
            value = value.astype(BF16)
            for_left[:, cols] = value[:SUB]
            for_right[:, cols] = value[SUB:]


def update_rows(place, left, root):
    strip = jax.ShapeDtypeStruct((SUB, BS), BF16)
    return pl.pallas_call(
        update_kernel,
        out_shape=[strip, strip],
        in_specs=[SMEM, VMEM, VMEM, VMEM],
        out_specs=[VMEM, VMEM],
        scratch_shapes=[pltpu.VMEM((2 * SUB, BS), BF16)] * 2,
        compiler_params=params(16),
        cost_estimate=cost(3 * 2 * 2 * SUB * BS * BS, 6 * 2**20),
        name="update_rows",
    )(place, left, *root)


def swap(value):
    return lax.ppermute(value, "dp", [(i, i ^ 1) for i in range(32)])


def along(value, step, y_core):
    pairs = []
    for source in range(32):
        z, y, core = source // 8, source // 2 % 4, source % 2
        if core == y_core:
            y = (y + step) % 4
        else:
            z = (z + step) % 4
        pairs.append((source, (z * 4 + y) * 2 + core))
    return lax.ppermute(value, "dp", pairs)


def body(activations, cotangent, owner_table, statistics, warm_roots):
    dp, group = lax.axis_index("dp"), lax.axis_index("group")
    core, y, z = dp % 2, dp // 2 % 4, dp // 8
    place = jnp.stack([z, y, core, group]).astype(jnp.int32)
    scale = 1.0 / math.sqrt(activations.shape[0] * lax.axis_size("dp"))

    sent = fetch_sent(place, activations)
    kept, cot = fetch_kept(place, activations, cotangent, sent)
    act_other, cot_other = swap(sent), swap(cot)
    out = partial_sums(scale, owner_table, place, kept, act_other, cot, cot_other)
    fifth = fifth_power(warm_roots[0], out[0])

    out = [out[0]] + [along(out[step], step, 0) for step in (2, 1, 3)]
    out = middle_sums(out, fifth[0])
    levels, *first = levels_of(fifth, statistics[0], warm_roots[0], out[0])
    out = [out[0]] + [along(out[step], step, 1) for step in (2, 1, 3)]
    piece = last_sums(out, levels)

    def around(value, step):
        return lax.ppermute(value, "group", [(i, (i + step) % 4) for i in range(4)])

    before, behind = around(piece, 1), around(piece, -1)
    pieces = [piece, before, behind, around(before[:SUB], 1), around(behind[SUB:], -1)]
    other = [swap(p) for p in pieces]

    outs = newton(place, pieces, other, statistics[0], warm_roots[0], levels, [fifth[0], *first])
    statistic, levels, last_fifth, stat, x, taken, left = outs[0], outs[1], outs[2:5], outs[5:8], *outs[8:]
    left = lax.ppermute(left, "dp", [(2 * k, 2 * k + 1) for k in range(16)])
    root, *root_parts = rest_of_root(place, levels, last_fifth, stat, x, taken)
    for_left, for_right = update_rows(place, left, root_parts)
    back = lax.ppermute(for_left, "dp", [(2 * k + 1, 2 * k) for k in range(16)])
    update = jnp.where(core == 0, back, for_right)
    return (statistic[None], root[None], update[None])


def solution(mesh):
    in_specs = (P("dp", None), P("dp", None), P(), P("dp", None, None), P("dp", None, None))
    out_specs = (P("dp", None, None), P("dp", None, None), P("dp", "group", None))
    return jax.shard_map(body, mesh=mesh, in_specs=in_specs, out_specs=out_specs, check_vma=False)
```
